256 devices in a mesh: dp: 2 (over core), mx: 16 (over y, x), my: 8 (over z).
Axes of the slice: x: 4, y: 4, z: 8, core: 2. Of those that a mesh axis runs over, the one named last changes fastest.
Arguments:
- patches: bfloat16 [1024, 6144], P('dp', 'mx'), may hold values from -40 to 40
- ln_gain: float32 [6144], P('mx'), may hold values from 0.5 to 2
- w_qkv: bfloat16 [3, 6144, 6144], P(None, 'mx', 'my'), may hold values from -1 to 1, as said below
- qk_gain: float32 [2, 6144], P(None, 'my'), may hold values from 0 to 6
- w_out: bfloat16 [6144, 6144], P('my', 'mx'), may hold values from -0.078125 to 0.078125
- w_up: bfloat16 [6144, 24576], P('mx', 'my'), may hold values from -0.078125 to 0.078125
- w_down: bfloat16 [24576, 6144], P('my', 'mx'), may hold values from -0.0390625 to 0.0390625
- w_adapt: bfloat16 [6144, 4096], P('mx', 'my'), may hold values from -0.078125 to 0.078125
- patch_counts: int32 [2, 2], P('dp'), may hold values from 1 to 256, 384 in all within a row
Outputs:
- encoded: bfloat16 [768, 4096], P(('dp', 'mx', 'my'))
The draws below stay inside these ranges and needn't reach their ends.
Inputs may be any that keep to these rules, and one draw needn't show every extreme that they name: `w_qkv`: entries scaled by the inverse square root of 6144.
All inputs are finite; a program needn't handle non-finite values.
Results may differ from the reference program's by a relative error of at most 0.027.
Values may be sent and summed in bfloat16 or wider, within the bound.
A program may use at most 64 MiB of HBM per device.

```python
import math
import jax
import jax.numpy as jnp
import numpy as np
from jax import lax

D = 6144
HEADS = 48
HD = 128
FF = 24576
E = 4096
PATCHES = 256
IMG_DP = 2
ROWS = 512
TOKENS = 1024
SLOTS_DP = 384
N_DP = 2
N_MX = 16


def draw_patches(key, part):
    key = jax.random.fold_in(key, 11)
    key_rows, key_cols, key_base = jax.random.split(key, 3)
    rows_scale = jnp.exp(jax.random.uniform(key_rows, (TOKENS, 1)) * jnp.log(10.0))
    column = jnp.arange(D).astype(jnp.float32) / D
    cols_scale = jnp.exp(column * jnp.log(3.0) + jax.random.uniform(key_cols, (D,)) * jnp.log(3.3))[None, :]
    base = jnp.clip(jax.random.normal(key_base, (TOKENS, D)), -4.0, 4.0)
    return (0.1 * base * rows_scale * cols_scale).astype(jnp.bfloat16)


def draw_w_qkv(key, part):
    key = jax.random.fold_in(key, 12)
    key_main = jax.random.fold_in(key, 0)
    scale = D ** (-0.5)
    base = jnp.clip(jax.random.normal(key_main, (3, D, D)), -4.0, 4.0) * scale
    return base.astype(jnp.bfloat16)


def draw_qk_gain(key, part):
    key = jax.random.fold_in(key, 13)
    key_head, key_chan = jax.random.split(key, 2)
    lowest, highest = (0.5, 1.6)
    strength = lowest * jnp.exp(jax.random.uniform(key_head, (2, HEADS, 1)) * jnp.log(highest / lowest))
    channel = 1.0 + 0.1 * jax.random.uniform(key_chan, (2, HEADS, HD), minval=-1.0, maxval=1.0)
    return (strength * channel).reshape(2, D).astype(jnp.float32)


def shard_levels(own_key, shape, cuts, least, largest):
    loudness, own = 1.0, jax.random.fold_in(own_key, 6)
    for axis_at, shards_of in cuts:
        steps = jnp.exp(jax.random.uniform(jax.random.fold_in(own, axis_at), (shards_of,), jnp.float32, least / len(cuts), largest / len(cuts)))
        loudness = loudness * jnp.repeat(steps, shape[axis_at] // shards_of).reshape([-1 if axis == axis_at else 1 for axis in range(len(shape))])
    return loudness


def profile(count, total, reach, lean):
    loads = [(1 << 20) // math.isqrt(rank ** lean) + 1 for rank in range(2, count + 1)]
    spare, given = total - reach - (count - 1), [1] * (count - 1)
    while spare > 0:
        candidates = [i for i in range(count - 1) if given[i] < reach]
        whole, budget = sum([loads[i] for i in candidates]), spare
        for i in candidates:
            extra = min(reach - given[i], max(1, budget * loads[i] // whole), spare)
            given[i] = given[i] + extra
            spare = spare - extra
    return np.array([reach] + given)


def uneven_parts(key, number_of, total, limit, skew):
    if number_of == 2:
        one = jax.random.randint(key, (), max(1, total - limit), min(limit, total - 1) + 1)
        return jnp.stack([one, total - one])
    lengths = jnp.asarray(profile(number_of, total, limit, skew), jnp.int32)
    pairs = (number_of - 1) // 2
    source_of, taker = lengths[1:1 + 2 * pairs:2], lengths[2:2 + 2 * pairs:2]
    slack = jnp.minimum(source_of - 1, limit - taker)
    shifted = jax.random.randint(jax.random.fold_in(key, 1), (pairs,), 0, 1 << 20) % (slack + 1)
    lengths = lengths.at[1:1 + 2 * pairs:2].set(source_of - shifted).at[2:2 + 2 * pairs:2].set(taker + shifted)
    return lengths[jax.random.permutation(jax.random.fold_in(key, 2), number_of)]


def bell_draw(own_key, dims, scale, limit, cuts=(), held_as=jnp.bfloat16):
    loudness = shard_levels(own_key, dims, cuts, -0.22, 0.18) if cuts else 1.0
    result = jax.random.normal(own_key, dims, jnp.float32) * scale * loudness
    return jnp.minimum(jnp.maximum(result, -limit), limit).astype(held_as)


def setup_inputs(seed: int = 0) -> dict:
    splits = jax.random.split(jax.random.key(seed), 10)
    patches = draw_patches(jax.random.fold_in(splits[9], 71), 0)
    ln_gain = jnp.clip(jnp.exp(math.log(2.0) - 1.3862944 * jax.random.uniform(splits[1], (D,), jnp.float32) ** shard_levels(splits[1], (D,), ((0, 16),), -0.2, 0.2)), 0.5, 2.0)
    w_qkv = draw_w_qkv(jax.random.fold_in(splits[9], 71), 0)
    qk_gain = draw_qk_gain(jax.random.fold_in(splits[9], 71), 0)
    w_out = bell_draw(splits[4], (D, D), D ** -0.5, 0.078125, ((0, 8), (1, 16)))
    w_up = bell_draw(splits[5], (D, FF), D ** -0.5, 0.078125, ((0, 16), (1, 8)))
    w_down = bell_draw(splits[6], (FF, D), FF ** -0.5, 0.0390625, ((0, 8), (1, 16)))
    w_adapt = bell_draw(splits[7], (D, E), D ** -0.5, 0.078125, ((0, 16), (1, 8)))
    patch_counts = jax.vmap(lambda own: uneven_parts(own, IMG_DP, SLOTS_DP, PATCHES, 1))(jax.random.split(splits[8], N_DP)).reshape((N_DP, IMG_DP)).astype(jnp.int32)
    return {"patches": patches, "ln_gain": ln_gain, "w_qkv": w_qkv, "qk_gain": qk_gain, "w_out": w_out, "w_up": w_up, "w_down": w_down, "w_adapt": w_adapt, "patch_counts": patch_counts}


def row_norm(values, gain):
    mean = lax.optimization_barrier(jnp.mean(values, -1, keepdims=True))
    square = lax.optimization_barrier(jnp.mean(values * values, -1, keepdims=True))
    return (values - mean) * lax.rsqrt(square - mean * mean + 1e-06) * gain

def blocked_sum(left, right):
    width = left.shape[1] // N_MX
    left_blocks = left.reshape(left.shape[0], N_MX, width).transpose(1, 0, 2)
    right_blocks = right.reshape(N_MX, width, right.shape[1])

    def step(total, pair):
        partial_value = jnp.dot(pair[0], pair[1], preferred_element_type=jnp.float32).astype(jnp.bfloat16)
        partial_value = lax.optimization_barrier(partial_value)
        return (total + partial_value.astype(jnp.float32), None)
    start = jnp.zeros((left.shape[0], right.shape[1]), jnp.float32)
    total, _ = lax.scan(step, start, (left_blocks, right_blocks))
    return total

def slot_sources(counts):
    counts = counts.astype(jnp.int32)
    ends = jnp.cumsum(counts).astype(jnp.int32)
    starts = (ends - counts).astype(jnp.int32)
    slot = jnp.arange(SLOTS_DP).astype(jnp.int32)
    image = lax.optimization_barrier(jnp.sum((ends[None, :] <= slot[:, None]).astype(jnp.int32), axis=1)).astype(jnp.int32)
    which = image[:, None] == jnp.arange(IMG_DP).astype(jnp.int32)[None, :]
    start = lax.optimization_barrier(jnp.sum(jnp.where(which, starts[None, :], 0), axis=1)).astype(jnp.int32)
    return (image * PATCHES + slot - start).astype(jnp.int32)

def reference(patches, ln_gain, w_qkv, qk_gain, w_out, w_up, w_down, w_adapt, patch_counts):
    results = []
    gains = qk_gain.reshape(2, HEADS, HD)
    for group in range(N_DP):
        tokens = patches[group * ROWS:(group + 1) * ROWS]
        tokens_f = tokens.astype(jnp.float32)
        normed = row_norm(tokens_f, ln_gain).astype(jnp.bfloat16)
        query_sum = blocked_sum(normed, w_qkv[0])
        key_sum = blocked_sum(normed, w_qkv[1])
        value_sum = blocked_sum(normed, w_qkv[2])
        lifted = blocked_sum(normed, w_up)
        queries = row_norm(query_sum.reshape(ROWS, HEADS, HD), gains[0]).astype(jnp.bfloat16)
        keys = row_norm(key_sum.reshape(ROWS, HEADS, HD), gains[1]).astype(jnp.bfloat16)
        values = value_sum.astype(jnp.bfloat16).reshape(ROWS, HEADS, HD)
        hidden = jax.nn.gelu(lifted, approximate=False).astype(jnp.bfloat16)
        query_img = queries.reshape(IMG_DP, PATCHES, HEADS, HD).astype(jnp.float32)
        key_img = keys.reshape(IMG_DP, PATCHES, HEADS, HD).astype(jnp.float32)
        value_img = values.reshape(IMG_DP, PATCHES, HEADS, HD).astype(jnp.float32)
        scores = jnp.einsum('iphd,iqhd->ihpq', query_img, key_img) * HD ** (-0.5)
        top = lax.optimization_barrier(jnp.max(scores, -1, keepdims=True))
        expo = jnp.exp(scores - top)
        weights = (expo / lax.optimization_barrier(jnp.sum(expo, -1, keepdims=True))).astype(jnp.bfloat16)
        attended = jnp.einsum('ihpq,iqhd->iphd', weights.astype(jnp.float32), value_img)
        attended = attended.astype(jnp.bfloat16).reshape(ROWS, D)
        branches = jnp.dot(attended, w_out, preferred_element_type=jnp.float32)
        branches = branches + jnp.dot(hidden, w_down, preferred_element_type=jnp.float32)
        updated = (tokens_f + branches).astype(jnp.bfloat16)
        adapted = jnp.dot(updated, w_adapt, preferred_element_type=jnp.float32)
        source = slot_sources(patch_counts[group])
        results.append(adapted[source].astype(jnp.bfloat16))
    return jnp.concatenate(results, axis=0)
```

```python
import jax
import jax.numpy as jnp
from jax import lax
from jax.experimental import pallas as pl
from jax.experimental.pallas import tpu as pltpu
from jax.sharding import PartitionSpec as P

MESH = pl.DeviceIdType.MESH
D = 6144
HD = 128
F32 = jnp.float32
BF16 = jnp.bfloat16

K0, V0, Q0, M0, UNITS = 0, 4, 8, 11, 23


def dot(a, b):
    return jnp.dot(a, b, preferred_element_type=F32)


def dot_t(a, b):
    return lax.dot_general(a, b, (((1,), (1,)), ((), ())), preferred_element_type=F32)


def kernel(
    x_hbm, gain_ref, wqkv_hbm, qkg_ref, wout_hbm, wup_hbm, wdown_hbm, wad_hbm, cnt_ref,
    out_ref,
    x, a, wv, wd, wa, stat, acc, snd, rcv, kv, qn, agb, zs, bsum, zr, xz, tr, fs, fr,
    sem_x, sem_wv, sem_wd, sem_wa,
    stat_s, stat_r, rs_s, rs_r, kv_s, kv_r, ag_s, ag_r, z_s, z_r, f_s, f_r, wz_s, wz_r, wc_s, wc_r,
):
    dp, mx, z = lax.axis_index("dp"), lax.axis_index("mx"), lax.axis_index("my")
    cy, cx = mx // 4, mx % 4
    vx, vy = cx // 2, cy // 2
    ux = cx % 2 + vx - 2 * (cx % 2) * vx
    uy = cy % 2 + vy - 2 * (cy % 2) * vy
    bits = (ux, uy, vx, vy)
    drow = ux * 4 + uy * 2 + vx
    halves = (vy, 1 - vy)

    def flip(c):
        return c + 1 - 2 * (c % 2)

    partners = (
        (dp, cy * 4 + flip(cx), z),
        (dp, flip(cy) * 4 + cx, z),
        (dp, cy * 4 + 3 - cx, z),
        (dp, (3 - cy) * 4 + cx, z),
    )
    plane = [((cy + o // 4) % 4) * 4 + (cx + o % 4) % 4 for o in range(1, 16)]
    column = [(z + o) % 8 for o in range(1, 8)]
    other = (1 - dp, mx, z)

    def relative(block):
        total = 0
        for bit, weight in ((block // 4, 4), ((block // 2) % 2, 2), (block % 2, 1)):
            own = bits[{4: 0, 2: 1, 1: 2}[weight]]
            total = total + weight * (bit + own - 2 * bit * own)
        return total

    sent = []

    def remote(src, dst, s, r, device):
        return pltpu.make_async_remote_copy(
            src_ref=src, dst_ref=dst, send_sem=s, recv_sem=r, device_id=device, device_id_type=MESH
        )

    def start(copy):
        copy.start()
        sent.append(copy)

    load_x = pltpu.make_async_copy(x_hbm, x, sem_x)
    load_x.start()
    load_wv, load_wd = {}, {}

    def half_at(base, half):
        return pl.ds(pl.multiple_of(base + half * 384, 128), 384)

    for i in (1, 2, 0, 3, 4, 5, 6):
        for h in range(2):
            if i < 3:
                src = wqkv_hbm.at[i, :, half_at(0, halves[h])]
            else:
                src = wup_hbm.at[:, half_at((i - 3) * 768, halves[h])]
            load_wv[i, h] = pltpu.make_async_copy(src, wv.at[i, h], sem_wv.at[i, h])
            load_wv[i, h].start()
    load_wa = pltpu.make_async_copy(wad_hbm, wa.at[z], sem_wa)
    load_wa.start()
    for i in range(5):
        for h in range(2):
            src = wdown_hbm.at[half_at(i * 768, halves[h])] if i < 4 else wout_hbm.at[half_at(0, halves[h])]
            load_wd[i, h] = pltpu.make_async_copy(src, wd.at[i, h], sem_wd.at[i, h])
            load_wd[i, h].start()

    barrier = pltpu.get_barrier_semaphore()
    greet = [(dp, m, z) for m in plane] + [(dp, mx, c) for c in column] + [other]
    for device in greet:
        pl.semaphore_signal(barrier, inc=1, device_id=device, device_id_type=MESH)

    load_x.wait()
    xb = x[...]
    xf = xb.astype(F32)
    x2 = xf * xf
    hi = x2.astype(BF16)
    lo = (x2 - hi.astype(F32)).astype(BF16)
    row8 = lax.broadcasted_iota(jnp.int32, (8, 384), 0)
    e0 = (row8 == 0).astype(F32).astype(BF16)
    e1 = (row8 == 1).astype(F32).astype(BF16)
    stat[0] = (dot_t(e0, xb) + dot_t(e1, hi) + dot_t(e1, lo))[0:2]

    pl.semaphore_wait(barrier, len(greet))
    for o in range(15):
        start(remote(stat.at[0], stat.at[o + 1], stat_s.at[o], stat_r, (dp, plane[o], z)))
    mine = pl.ds(pl.multiple_of(dp * 192, 16), 192)
    for o in range(7):
        start(remote(wad_hbm.at[mine], wa.at[z, mine], wz_s.at[o], wz_r, (dp, mx, column[o])))

    c0 = cnt_ref[0, 0]

    def pick(slot, width):
        token = slot + jnp.where(slot >= c0, 256 - c0, 0)
        lane = lax.broadcasted_iota(jnp.int32, token.shape, 1)
        parts = [
            jnp.where(token == lane + 128 * j, 1.0, 0.0).astype(BF16) for j in range(width // 128)
        ]
        return jnp.concatenate(parts, axis=1)

    row = lax.broadcasted_iota(jnp.int32, (384, 128), 0)
    block = jnp.bitwise_xor((row >> 4) & 7, drow)
    chosen = pick((row & 15) * 24 + block * 3 + (row >> 7), 512)
    row = lax.broadcasted_iota(jnp.int32, (48, 128), 0)
    own_z = pick((row & 15) * 24 + z * 3 + (row >> 4), 512)
    xz[...] = dot(own_z, xb)

    remote(stat.at[pl.ds(1, 15)], stat.at[pl.ds(1, 15)], stat_s.at[0], stat_r, partners[0]).wait_recv()
    total = stat[0]
    for o in range(1, 16):
        total = total + stat[o]
    total = total * (1.0 / D)
    mean, square = total[0:1], total[1:2]
    scale = lax.rsqrt(square - mean * mean + 1e-06)
    mean_t = jnp.transpose(jnp.broadcast_to(mean, (128, 512)))
    scale_t = jnp.transpose(jnp.broadcast_to(scale, (128, 512)))
    gain = gain_ref[...]
    normed = jnp.concatenate(
        [
            ((xf[:, j * 128:(j + 1) * 128] - mean_t) * scale_t * gain[:, j * 128:(j + 1) * 128]).astype(BF16)
            for j in range(3)
        ],
        axis=1,
    )
    for b in range(8):
        place = relative(b)
        for g in range(4):
            a[g, place] = normed[g * 128 + b * 16:g * 128 + b * 16 + 16]
    for k in range(3):
        a[4 + k] = dot(chosen[k * 128:(k + 1) * 128], normed).astype(BF16).reshape(8, 16, 384)

    def offset(t):
        return 16 - (16 >> t)

    def rs_copy(u, c, t):
        at = pl.ds(offset(t), 8 >> t)
        return remote(snd.at[u, at], rcv.at[u, at], rs_s.at[u, t], rs_r.at[u, t], partners[(c + t) % 4])

    def place_of(c, b, h):
        own = ((b >> 2) & 1, (b >> 1) & 1, b & 1, h)
        return sum(own[(c + t) % 4] << (3 - t) for t in range(4))

    loaded = set()

    def product(u, rows, w, c):
        left = a[rows].reshape(128, 384)
        for h in range(2):
            if (w, h) not in loaded:
                load_wv[w, h].wait()
                loaded.add((w, h))
            value = dot(left, wv[w, h])
            for b in range(8):
                j = place_of(c, b, h)
                part = value[b * 16:(b + 1) * 16]
                if j >= 8:
                    snd[u, j - 8] = part.astype(BF16)
                else:
                    acc[u, j] = part
        start(rs_copy(u, c, 0))

    def rs_step(u, c, t):
        rs_copy(u, c, t - 1).wait_recv()
        half, at, to = 4 >> (t - 1), offset(t - 1), offset(t)
        snd[u, pl.ds(to, half)] = (
            acc[u, pl.ds(half, half)] + rcv[u, pl.ds(at + half, half)].astype(F32)
        ).astype(BF16)
        start(rs_copy(u, c, t))
        acc[u, pl.ds(0, half)] = acc[u, pl.ds(0, half)] + rcv[u, pl.ds(at, half)].astype(F32)

    def rs_last(u, c):
        rs_copy(u, c, 3).wait_recv()
        return acc[u, 0] + rcv[u, 14].astype(F32)

    head_gain = qkg_ref[:, half_at(0, vy)]

    def head_norm(value, which):
        parts = []
        for h in range(3):
            cut = slice(h * HD, (h + 1) * HD)
            v = value[:, cut]
            mean = jnp.mean(v, -1, keepdims=True)
            square = jnp.mean(v * v, -1, keepdims=True)
            parts.append((v - mean) * lax.rsqrt(square - mean * mean + 1e-06) * head_gain[which:which + 1, cut])
        return jnp.concatenate(parts, axis=1).astype(BF16)

    def kv_copy(c, s):
        n = 1 << s
        return remote(
            kv.at[c, pl.ds(0, n)], kv.at[c, pl.ds(n, n)], kv_s.at[c, s], kv_r.at[c, s], partners[(c + s) % 3]
        )

    def ag_copy(k, i, s):
        n, c = 1 << s, (i if i < 4 else k)
        return remote(
            agb.at[k, i, pl.ds(0, n)], agb.at[k, i, pl.ds(n, n)], ag_s.at[k, i, s], ag_r.at[k, i, s],
            partners[(c + 3 - s) % 4],
        )

    def ag_step(k, i, s):
        if s > 0:
            ag_copy(k, i, s - 1).wait_recv()
        if s < 4:
            start(ag_copy(k, i, s))

    def k_last(c):
        kv[c, 0, pl.ds(0, 16)] = head_norm(rs_last(K0 + c, c), 1)

    def v_last(c):
        kv[c, 0, pl.ds(16, 16)] = rs_last(V0 + c, c).astype(BF16)
        start(kv_copy(c, 0))

    def q_last(c):
        qn[c] = head_norm(rs_last(Q0 + c, c), 0)

    def m_last(k, c):
        value = rs_last(M0 + 4 * k + c, c)
        agb[k, c, 0] = (0.5 * value * (1.0 + lax.erf(value * (0.5 ** 0.5)))).astype(BF16)
        ag_step(k, c, 0)

    def kv_step(c, s):
        kv_copy(c, s - 1).wait_recv()
        if s < 3:
            start(kv_copy(c, s))

    def attention():
        row = lax.broadcasted_iota(jnp.int32, (48, HD), 0)
        first = (row & 15) * 24 + drow * 3 + (row >> 4) < c0
        queries = qn[...].reshape(48, 384)
        for h in range(3):
            cut = slice(h * HD, (h + 1) * HD)
            found = []
            for image in range(2):
                held = kv[pl.ds(2 * image, 2), :, :, cut]
                keys = held[:, :, 0:16].reshape(256, HD)
                values = held[:, :, 16:32].reshape(256, HD)
                scores = dot_t(queries[:, cut], keys) * HD ** (-0.5)
                expo = jnp.exp(scores - jnp.max(scores, -1, keepdims=True))
                weights = (expo / jnp.sum(expo, -1, keepdims=True)).astype(BF16)
                found.append(dot(weights, values))
            attended = jnp.where(first, found[0], found[1]).astype(BF16)
            for k in range(3):
                agb[k, 4, 0, :, cut] = attended[k * 16:(k + 1) * 16]
        for k in range(3):
            ag_step(k, 4, 0)

    def branch(k):
        value = None
        for i in range(5):
            c = i if i < 4 else k
            for h in range(2):
                left = jnp.concatenate([agb[k, i, place_of(c, b, h)] for b in range(8)], axis=0)
                if k == 0:
                    load_wd[i, h].wait()
                part = dot(left, wd[i, h])
                value = part if value is None else value + part
        bsum[k] = value.reshape(8, 16, 384)
        zs[k] = value.astype(BF16).reshape(8, 16, 384)
        for o in range(7):
            src = zs.at[k, relative(column[o])]
            start(remote(src, zr.at[k, o], z_s.at[k, o], z_r.at[k], (dp, mx, column[o])))

    def adapt(k):
        remote(zr.at[k], zr.at[k], z_s.at[k, 0], z_r.at[k], (dp, mx, column[0])).wait_recv()
        value = bsum[k, relative(z)]
        for o in range(7):
            value = value + zr[k, o].astype(F32)
        updated = (xz[pl.ds(k * 16, 16)] + value).astype(BF16)
        for b in range(8):
            part = dot(updated, wa[b])
            for j in range(4):
                tr[k, pl.ds(b * 4 + j, 16, stride=32), :] = part[:, j * 128:(j + 1) * 128]
        fs[k] = tr[k].astype(BF16).reshape(16, 32, 128)
        for o in range(15):
            start(remote(fs.at[k, plane[o]], fr.at[k, o], f_s.at[k, o], f_r.at[k], (dp, plane[o], z)))

    def finish(k):
        remote(fr.at[k], fr.at[k], f_s.at[k, 0], f_r.at[k], (dp, plane[0], z)).wait_recv()
        value = tr[k, pl.ds(pl.multiple_of(mx * 32, 32), 32)]
        for o in range(15):
            value = value + fr[k, o].astype(F32)
        out_ref[k] = value.astype(BF16)

    def adapter_across():
        load_wa.wait()
        some = wa.at[pl.ds(0, 7), pl.ds(0, 192)]
        remote(some, some, wz_s.at[0], wz_r, (dp, mx, column[0])).wait_recv()
        for o in range(7):
            at = wa.at[column[o], mine]
            start(remote(at, at, wc_s.at[o], wc_r, other))

    def adapter_ready():
        some = wa.at[pl.ds(0, 7), pl.ds(0, 192)]
        remote(some, some, wc_s.at[0], wc_r, other).wait_recv()

    four, three = range(4), range(3)

    def wave(first, count, t):
        for c in range(count):
            rs_step(first + c, c, t)

    def up(k):
        for c in four:
            product(M0 + 4 * k + c, 4 + k, 3 + c, c)

    def m_step(k, t):
        wave(M0 + 4 * k, 4, t)

    def m_end(k):
        for c in four:
            m_last(k, c)

    def gather(k, s):
        for c in four:
            ag_step(k, c, s)

    def gather_attended(s):
        for k in three:
            ag_step(k, 4, s)

    for c in four:
        product(K0 + c, c, 1, c)
    for c in four:
        product(V0 + c, c, 2, c)
    for c in three:
        product(Q0 + c, 4 + c, 0, c)
    wave(K0, 4, 1)
    wave(V0, 4, 1)
    up(0)
    wave(Q0, 3, 1)
    wave(K0, 4, 2)
    wave(V0, 4, 2)
    up(1)
    m_step(0, 1)
    wave(Q0, 3, 2)
    wave(K0, 4, 3)
    wave(V0, 4, 3)
    up(2)
    for c in four:
        k_last(c)
    for c in four:
        v_last(c)
    m_step(1, 1)
    m_step(0, 2)
    wave(Q0, 3, 3)
    for c in four:
        kv_step(c, 1)
    m_step(2, 1)
    m_step(1, 2)
    m_step(0, 3)
    for c in three:
        q_last(c)
    for c in four:
        kv_step(c, 2)
    m_step(2, 2)
    m_step(1, 3)
    m_end(0)
    for c in four:
        kv_step(c, 3)
    attention()
    m_step(2, 3)
    m_end(1)
    gather(0, 1)
    adapter_across()
    m_end(2)
    gather_attended(1)
    gather(0, 2)
    gather(1, 1)
    gather_attended(2)
    gather(0, 3)
    gather(1, 2)
    gather(2, 1)
    gather_attended(3)
    gather(1, 3)
    gather(2, 2)
    gather(0, 4)
    gather_attended(4)
    branch(0)
    gather(2, 3)
    gather(1, 4)
    branch(1)
    adapter_ready()
    adapt(0)
    gather(2, 4)
    branch(2)
    adapt(1)
    adapt(2)
    for k in three:
        finish(k)
    for copy in sent:
        copy.wait_send()


def per_device(patches, ln_gain, w_qkv, qk_gain, w_out, w_up, w_down, w_adapt, patch_counts):
    vmem, hbm = pl.BlockSpec(memory_space=pltpu.VMEM), pl.BlockSpec(memory_space=pl.ANY)
    dma = pltpu.SemaphoreType.DMA
    out = pl.pallas_call(
        kernel,
        out_shape=jax.ShapeDtypeStruct((3, 32, 128), BF16),
        in_specs=[hbm, vmem, hbm, vmem, hbm, hbm, hbm, hbm, pl.BlockSpec(memory_space=pltpu.SMEM)],
        out_specs=vmem,
        scratch_shapes=[
            pltpu.VMEM((512, 384), BF16),
            pltpu.VMEM((7, 8, 16, 384), BF16),
            pltpu.VMEM((7, 2, 384, 384), BF16),
            pltpu.VMEM((5, 2, 384, 384), BF16),
            pltpu.VMEM((8, 384, 512), BF16),
            pltpu.VMEM((16, 2, 512), F32),
            pltpu.VMEM((UNITS, 8, 16, 384), F32),
            pltpu.VMEM((UNITS, 15, 16, 384), BF16),
            pltpu.VMEM((UNITS, 15, 16, 384), BF16),
            pltpu.VMEM((4, 8, 32, 384), BF16),
            pltpu.VMEM((3, 16, 384), BF16),
            pltpu.VMEM((3, 5, 16, 16, 384), BF16),
            pltpu.VMEM((3, 8, 16, 384), BF16),
            pltpu.VMEM((3, 8, 16, 384), F32),
            pltpu.VMEM((3, 7, 16, 384), BF16),
            pltpu.VMEM((48, 384), F32),
            pltpu.VMEM((3, 512, 128), F32),
            pltpu.VMEM((3, 16, 32, 128), BF16),
            pltpu.VMEM((3, 15, 32, 128), BF16),
            dma, dma((7, 2)), dma((5, 2)), dma,
            dma((15,)), dma,
            dma((UNITS, 4)), dma((UNITS, 4)),
            dma((4, 3)), dma((4, 3)),
            dma((3, 5, 4)), dma((3, 5, 4)),
            dma((3, 7)), dma((3,)),
            dma((3, 15)), dma((3,)),
            dma((7,)), dma,
            dma((7,)), dma,
        ],
        compiler_params=pltpu.CompilerParams(
            collective_id=0, has_side_effects=True, vmem_limit_bytes=48 * 2**20
        ),
    )(patches, ln_gain.reshape(1, 384), w_qkv, qk_gain, w_out, w_up, w_down, w_adapt, patch_counts)
    return out.reshape(3, 4096)


def solution(mesh):
    return jax.shard_map(
        per_device,
        mesh=mesh,
        in_specs=(
            P("dp", "mx"),
            P("mx"),
            P(None, "mx", "my"),
            P(None, "my"),
            P("my", "mx"),
            P("mx", "my"),
            P("my", "mx"),
            P("mx", "my"),
            P("dp", None),
        ),
        out_specs=P(("dp", "mx", "my"), None),
        check_vma=False,
    )
```

```python
import jax
import jax.numpy as jnp
from jax import lax
from jax.experimental import pallas as pl
from jax.experimental.pallas import tpu as pltpu
from jax.sharding import PartitionSpec as P

MESH = pl.DeviceIdType.MESH
D = 6144
HD = 128
F32 = jnp.float32
BF16 = jnp.bfloat16

K0, V0, Q0, M0, UNITS = 0, 4, 8, 11, 23
Q_CLASS, A_CLASS = (3, 0, 2), (3, 1, 2)
UNIT = (
    [(c, 1, c) for c in range(4)]
    + [(c, 2, c) for c in range(4)]
    + [(4 + k, 0, Q_CLASS[k]) for k in range(3)]
    + [(4 + k, 3 + c, c) for k in range(3) for c in range(4)]
)
KV_LINKS = ((0, 1, 2), (1, 2, 0), (2, 0, 1), (2, 1, 0))
FIRST = (3, 0, 1, 2)

ORDER = (
    ("ch",), ("x",), ("greet",), ("p", 6), ("s", 0), ("c", 0), ("p", 5), ("p", 2), ("p", 7), ("p", 4), ("s", 1),
    ("w", 0), ("p", 1), ("p", 17), ("p", 3), ("r", 6, 1), ("c", 1), ("p", 0), ("p", 12), ("p", 13), ("r", 5, 1),
    ("r", 2, 1), ("p", 15), ("r", 7, 1), ("r", 4, 1), ("s", 2), ("c", 2), ("p", 8), ("r", 1, 1), ("r", 17, 1),
    ("r", 3, 1), ("w", 1), ("p", 21), ("r", 0, 1), ("r", 6, 2), ("r", 12, 1), ("r", 13, 1), ("p", 20), ("r", 2, 2),
    ("r", 4, 2), ("r", 5, 2), ("s", 3), ("p", 9), ("r", 15, 1), ("p", 22), ("r", 1, 2), ("c", 3), ("r", 7, 2),
    ("r", 8, 1), ("r", 0, 2), ("r", 3, 2), ("r", 17, 2), ("r", 6, 3), ("r", 21, 1), ("r", 2, 3), ("r", 13, 2),
    ("p", 16), ("r", 5, 3), ("r", 12, 2), ("r", 20, 1), ("w", 2), ("p", 19), ("r", 4, 3), ("p", 18), ("s", 4),
    ("r", 15, 2), ("r", 9, 1), ("r", 7, 3), ("r", 22, 1), ("r", 3, 3), ("r", 8, 2), ("r", 1, 3), ("p", 10),
    ("r", 17, 3), ("p", 14), ("c", 4), ("n",), ("r", 16, 1), ("r", 0, 3), ("p", 11), ("e", 6), ("r", 15, 3), ("e", 5),
    ("r", 19, 1), ("r", 20, 2), ("e", 7), ("e", 3), ("v", 3, 0), ("r", 9, 2), ("e", 4), ("e", 2), ("v", 2, 0),
    ("r", 21, 2), ("r", 18, 1), ("e", 1), ("v", 1, 0), ("r", 22, 2), ("r", 8, 3), ("r", 12, 3), ("r", 13, 3),
    ("e", 17), ("w", 3), ("r", 10, 1), ("r", 14, 1), ("e", 0), ("v", 0, 0), ("e", 15), ("r", 16, 2), ("r", 19, 2),
    ("r", 20, 3), ("v", 3, 1), ("r", 11, 1), ("r", 9, 3), ("v", 1, 1), ("r", 21, 3), ("v", 2, 1), ("r", 22, 3),
    ("e", 8), ("e", 13), ("g", 1, 2, 1), ("r", 18, 2), ("e", 12), ("r", 10, 2), ("g", 1, 0, 1), ("r", 19, 3),
    ("r", 16, 3), ("r", 14, 2), ("e", 9), ("v", 3, 2), ("v", 0, 1), ("e", 20), ("v", 1, 2), ("e", 22), ("r", 11, 2),
    ("e", 21), ("v", 2, 2), ("g", 0, 2, 1), ("w", 4), ("g", 1, 0, 2), ("e", 19), ("r", 18, 3), ("g", 1, 2, 2),
    ("g", 0, 1, 1), ("r", 14, 3), ("r", 10, 3), ("e", 16), ("v", 0, 2), ("g", 2, 3, 1), ("g", 2, 2, 1), ("r", 11, 3),
    ("g", 2, 0, 1), ("e", 18), ("v", 3, 3), ("e", 14), ("g", 2, 1, 1), ("g", 1, 2, 3), ("v", 2, 3), ("g", 0, 1, 2),
    ("e", 11), ("g", 1, 0, 3), ("v", 1, 3), ("e", 10), ("g", 0, 2, 2), ("g", 2, 3, 2), ("v", 0, 3), ("att",),
    ("g", 1, 1, 1), ("g", 1, 3, 1), ("g", 0, 0, 1), ("g", 0, 3, 1), ("g", 2, 1, 2), ("g", 2, 0, 2), ("g", 2, 2, 2),
    ("b", 1, 2), ("g", 0, 2, 3), ("b", 1, 0), ("g", 0, 1, 3), ("g", 2, 4, 1), ("g", 0, 4, 1), ("g", 2, 3, 3),
    ("g", 1, 1, 2), ("g", 1, 4, 1), ("g", 0, 0, 2), ("g", 1, 3, 2), ("g", 0, 3, 2), ("g", 2, 2, 3), ("g", 2, 1, 3),
    ("g", 2, 0, 3), ("g", 2, 4, 2), ("b", 0, 2), ("g", 1, 3, 3), ("b", 0, 1), ("b", 2, 3), ("g", 0, 4, 2),
    ("g", 1, 1, 3), ("g", 0, 3, 3), ("g", 1, 4, 2), ("g", 0, 0, 3), ("g", 2, 4, 3), ("b", 2, 2), ("b", 2, 0),
    ("b", 2, 1), ("g", 0, 4, 3), ("b", 1, 3), ("g", 1, 4, 3), ("b", 1, 1), ("b", 0, 0), ("b", 0, 3), ("b", 2, 4),
    ("z", 2), ("b", 0, 4), ("z", 0), ("b", 1, 4), ("z", 1), ("a", 2), ("a", 0), ("d",), ("a", 1), ("f", 2), ("f", 0),
    ("f", 1),
)


def dot(a, b):
    return jnp.dot(a, b, preferred_element_type=F32)


def dot_t(a, b):
    return lax.dot_general(a, b, (((1,), (1,)), ((), ())), preferred_element_type=F32)


def kernel(
    x_hbm, gain_ref, wqkv_hbm, qkg_ref, wout_hbm, wup_hbm, wdown_hbm, wad_hbm, cnt_ref,
    out_ref,
    x, a, wv, wd, wa, stat, cpk, cr, tt, corr, rst, acc, snd, rcv, kv, qn, agb, zs, bsum, zr, xz, tr, fs, fr,
    sem_x, sem_wv, sem_wd, sem_wa,
    stat_s, stat_r, c_s, c_r, rs_s, rs_r, kv_s, kv_r, ag_s, ag_r, z_s, z_r, f_s, f_r, wz_s, wz_r, wc_s, wc_r,
):
    dp, mx, z = lax.axis_index("dp"), lax.axis_index("mx"), lax.axis_index("my")
    cy, cx = mx // 4, mx % 4
    vx, vy = cx // 2, cy // 2
    ux = cx % 2 + vx - 2 * (cx % 2) * vx
    uy = cy % 2 + vy - 2 * (cy % 2) * vy
    bits = (ux, uy, vx, vy)
    drow = ux * 4 + uy * 2 + vx
    halves = (vy, 1 - vy)

    def flip(c):
        return c + 1 - 2 * (c % 2)

    partners = (
        (dp, cy * 4 + flip(cx), z),
        (dp, flip(cy) * 4 + cx, z),
        (dp, cy * 4 + 3 - cx, z),
        (dp, (3 - cy) * 4 + cx, z),
    )
    plane = [((cy + o // 4) % 4) * 4 + (cx + o % 4) % 4 for o in range(1, 16)]
    column = [(z + o) % 8 for o in range(1, 8)]
    other = (1 - dp, mx, z)

    def relative(block):
        total = 0
        for bit, weight in ((block // 4, 4), ((block // 2) % 2, 2), (block % 2, 1)):
            own = bits[{4: 0, 2: 1, 1: 2}[weight]]
            total = total + weight * (bit + own - 2 * bit * own)
        return total

    sent = []

    def remote(src, dst, s, r, device):
        return pltpu.make_async_remote_copy(
            src_ref=src, dst_ref=dst, send_sem=s, recv_sem=r, device_id=device, device_id_type=MESH
        )

    def start(copy):
        copy.start()
        sent.append(copy)

    barrier = pltpu.get_barrier_semaphore()
    for device in partners + ((dp, mx, column[0]), (dp, mx, column[6]), other):
        pl.semaphore_signal(barrier, inc=1, device_id=device, device_id_type=MESH)

    load_x = pltpu.make_async_copy(x_hbm, x, sem_x)
    load_x.start()
    load_wv, load_wd = {}, {}

    def half_at(base, half):
        return pl.ds(pl.multiple_of(base + half * 384, 128), 384)

    for i in (1, 2, 0, 3, 4, 5, 6):
        for h in range(2):
            if i < 3:
                src = wqkv_hbm.at[i, :, half_at(0, halves[h])]
            else:
                src = wup_hbm.at[:, half_at((i - 3) * 768, halves[h])]
            load_wv[i, h] = pltpu.make_async_copy(src, wv.at[i, h], sem_wv.at[i, h])
            load_wv[i, h].start()
    load_wa = pltpu.make_async_copy(wad_hbm, wa.at[z], sem_wa)
    load_wa.start()
    for i in range(5):
        for h in range(2):
            src = wdown_hbm.at[half_at(i * 768, halves[h])] if i < 4 else wout_hbm.at[half_at(0, halves[h])]
            load_wd[i, h] = pltpu.make_async_copy(src, wd.at[i, h], sem_wd.at[i, h])
            load_wd[i, h].start()

    mine = pl.ds(pl.multiple_of(dp * 192, 16), 192)

    def ring_copy(way, s):
        block, to = ((z + 8 - s) % 8, (z + 1) % 8) if way == 0 else ((z + s) % 8, (z + 7) % 8)
        src = wad_hbm.at[mine] if s == 0 else wa.at[block, mine]
        i = way * 4 + s
        return remote(src, wa.at[block, mine], wz_s.at[i], wz_r.at[i], (dp, mx, to))

    def across_copy(way, s):
        block = (z + 8 - s) % 8 if way == 0 else (z + s) % 8
        i = way * 4 + s - 1
        return remote(wa.at[block, mine], wa.at[block, mine], wc_s.at[i], wc_r.at[i], other)

    def ring_step(s):
        for way in range(2):
            steps = 4 - way
            if 0 < s <= steps:
                ring_copy(way, s - 1).wait_recv()
            if s < steps:
                start(ring_copy(way, s))
            if 0 < s <= steps:
                start(across_copy(way, s))

    load_x.wait()
    xb = x[...]
    xf = xb.astype(F32)
    gain = gain_ref[...]
    centred = ((xf - jnp.mean(xf, -1, keepdims=True)) * gain).astype(BF16)
    for b in range(8):
        place = relative(b)
        for g in range(4):
            a[g, place] = centred[g * 128 + b * 16:g * 128 + b * 16 + 16]

    c0 = cnt_ref[0, 0]

    def pick(slot):
        token = slot + jnp.where(slot >= c0, 256 - c0, 0)
        lane = lax.broadcasted_iota(jnp.int32, token.shape, 1)
        return jnp.concatenate([jnp.where(token == lane + 128 * j, 1.0, 0.0).astype(BF16) for j in range(4)], axis=1)

    def choose():
        row = lax.broadcasted_iota(jnp.int32, (384, 128), 0)
        block = jnp.bitwise_xor((row >> 4) & 7, drow)
        chosen = pick((row & 15) * 24 + block * 3 + (row >> 7))
        for k in range(3):
            a[4 + k] = dot(chosen[k * 128:(k + 1) * 128], centred).astype(BF16).reshape(8, 16, 384)

    loaded = set()

    def weights(w, h):
        if (w, h) not in loaded:
            load_wv[w, h].wait()
            loaded.add((w, h))
        return wv[w, h]

    def stat_copy(s):
        n = 1 << s
        return remote(stat.at[pl.ds(0, n)], stat.at[pl.ds(n, n)], stat_s.at[s], stat_r.at[s], partners[FIRST[s]])

    def stat_step(s):
        if s == 0:
            row8 = lax.broadcasted_iota(jnp.int32, (8, 384), 0)
            e0, e1 = (row8 == 0).astype(F32).astype(BF16), (row8 == 1).astype(F32).astype(BF16)
            x2 = xf * xf
            hi = x2.astype(BF16)
            lo = (x2 - hi.astype(F32)).astype(BF16)
            stat[0] = (dot_t(e0, xb) + dot_t(e1, hi) + dot_t(e1, lo))[0:2]
        else:
            stat_copy(s - 1).wait_recv()
        if s < 4:
            start(stat_copy(s))

    def split(value):
        hi = value.astype(BF16).astype(F32)
        return hi, (value - hi).astype(BF16).astype(F32)

    def c_copy(s):
        if s == 0:
            src, dst = cpk, cr.at[1]
        else:
            n = 1 << s
            src, dst = cr.at[pl.ds(0, n)], cr.at[pl.ds(n, n)]
        return remote(src, dst, c_s.at[s], c_r.at[s], partners[FIRST[s]])

    def c_step(s):
        if s == 0:
            g0, rest = split(gain)
            g1, g2 = split(gain - g0)
            row24 = lax.broadcasted_iota(jnp.int32, (24, 384), 0)
            parts = jnp.where(row24 < 8, g0, jnp.where(row24 < 16, g1, g2))
            for h in (1, 0):
                value = None
                for w in range(7):
                    left = jnp.where((row24 & 7) == w, parts, 0.0).astype(BF16)
                    part = dot(left, weights(w, h))
                    value = part if value is None else value + part
                sums = jnp.concatenate(split(value[0:8] + value[8:16] + value[16:24]), axis=0).astype(BF16)
                if h == 1:
                    cpk[...] = sums
                else:
                    cr[0] = sums
        else:
            c_copy(s - 1).wait_recv()
        if s < 4:
            start(c_copy(s))

    def correct():
        sums = jnp.concatenate([stat[j][0:1] for j in range(16)], axis=0)
        squares = jnp.concatenate([stat[j][1:2] for j in range(16)], axis=0)
        mean = jnp.sum(sums, 0, keepdims=True) * (1.0 / D)
        square = jnp.sum(squares, 0, keepdims=True) * (1.0 / D)
        scale = lax.rsqrt(square - mean * mean + 1e-06)
        hi, lo = split(sums * (1.0 / 384) - mean)
        s0, rest = split(scale)
        s1, s2 = split(scale - s0)
        row8 = lax.broadcasted_iota(jnp.int32, (8, 512), 0)
        scales = jnp.where(row8 == 0, s0, jnp.where(row8 == 1, s1, jnp.where(row8 == 2, s2, 0.0)))
        table = jnp.concatenate([hi, lo, scales, jnp.zeros((88, 512), F32)], axis=0)
        table = jnp.transpose(table).astype(BF16)
        tt[...] = table.reshape(4, 8, 16, 128)
        row = lax.broadcasted_iota(jnp.int32, (48, 128), 0)
        own = dot(pick((row & 15) * 24 + drow * 3 + (row >> 4)), table).astype(BF16)
        rows = [tt[r, drow] if r < 4 else own[(r - 4) * 16:(r - 3) * 16] for r, w, c in UNIT]
        left = jnp.concatenate(rows, axis=0)
        j = lax.broadcasted_iota(jnp.int32, (128, 256), 0)
        lane = lax.broadcasted_iota(jnp.int32, (128, 256), 1)
        spread_hi = jnp.where((lane >> 4) == j, 1.0, 0.0).astype(BF16)
        spread_lo = jnp.where((lane >> 4) + 16 == j, 1.0, 0.0).astype(BF16)
        j = lax.broadcasted_iota(jnp.int32, (128, 128), 0)
        spread_scale = jnp.where((j >= 32) & (j < 35), 1.0, 0.0).astype(BF16)
        rst[...] = dot(left, spread_scale).reshape(UNITS, 16, 128)
        unit = lax.broadcasted_iota(jnp.int32, (UNITS * 16, 256), 0) >> 4
        group = jnp.where(unit < V0, 1, jnp.where(unit < Q0, 2, jnp.where(unit < M0, 0, 3 + ((unit - M0) & 3))))
        at = lax.broadcasted_iota(jnp.int32, (UNITS * 16, 256), 1) & 15
        left_hi = jnp.where((at & 7) == group, dot(left, spread_hi), 0.0).astype(BF16)
        left_lo = jnp.where(at == group, dot(left, spread_lo), 0.0).astype(BF16)
        held = cr[...].reshape(256, 384)
        corr[...] = (dot(left_hi, held) + dot(left_lo, held)).reshape(UNITS, 16, 384)

    def offset(t):
        return 16 - (16 >> t)

    def rs_copy(u, c, t):
        at = pl.ds(offset(t), 8 >> t)
        return remote(snd.at[u, at], rcv.at[u, at], rs_s.at[u, t], rs_r.at[u, t], partners[(c + t) % 4])

    def place_of(c, b, h):
        own = ((b >> 2) & 1, (b >> 1) & 1, b & 1, h)
        return sum(own[(c + t) % 4] << (3 - t) for t in range(4))

    def product(u):
        rows, w, c = UNIT[u]
        left = a[rows].reshape(128, 384)
        for h in range(2):
            value = dot(left, weights(w, h))
            for b in range(8):
                j = place_of(c, b, h)
                part = value[b * 16:(b + 1) * 16]
                if j >= 8:
                    snd[u, j - 8] = part.astype(BF16)
                else:
                    acc[u, j] = part
        start(rs_copy(u, c, 0))

    def rs_step(u, t):
        c = UNIT[u][2]
        rs_copy(u, c, t - 1).wait_recv()
        half, at, to = 4 >> (t - 1), offset(t - 1), offset(t)
        snd[u, pl.ds(to, half)] = (
            acc[u, pl.ds(half, half)] + rcv[u, pl.ds(at + half, half)].astype(F32)
        ).astype(BF16)
        start(rs_copy(u, c, t))
        acc[u, pl.ds(0, half)] = acc[u, pl.ds(0, half)] + rcv[u, pl.ds(at, half)].astype(F32)

    def rs_last(u):
        rs_copy(u, UNIT[u][2], 3).wait_recv()
        value = acc[u, 0] + rcv[u, 14].astype(F32) + corr[u]
        return value * jnp.concatenate([rst[u]] * 3, axis=1)

    head_gain = qkg_ref[:, half_at(0, vy)]

    def head_norm(value, which):
        parts = []
        for h in range(3):
            cut = slice(h * HD, (h + 1) * HD)
            v = value[:, cut]
            mean = jnp.mean(v, -1, keepdims=True)
            square = jnp.mean(v * v, -1, keepdims=True)
            parts.append((v - mean) * lax.rsqrt(square - mean * mean + 1e-06) * head_gain[which:which + 1, cut])
        return jnp.concatenate(parts, axis=1).astype(BF16)

    def kv_copy(c, s):
        n = 1 << s
        return remote(
            kv.at[c, pl.ds(0, n)], kv.at[c, pl.ds(n, n)], kv_s.at[c, s], kv_r.at[c, s], partners[KV_LINKS[c][s]]
        )

    def ag_copy(k, i, s):
        n, c = 1 << s, (i if i < 4 else A_CLASS[k])
        return remote(
            agb.at[k, i, pl.ds(0, n)], agb.at[k, i, pl.ds(n, n)], ag_s.at[k, i, s], ag_r.at[k, i, s],
            partners[(c + 3 - s) % 4],
        )

    def ag_step(k, i, s):
        if s > 0:
            ag_copy(k, i, s - 1).wait_recv()
        if s < 4:
            start(ag_copy(k, i, s))

    def rs_end(u):
        value = rs_last(u)
        if u < V0:
            kv[u, 0, pl.ds(0, 16)] = head_norm(value, 1)
        elif u < Q0:
            kv[u - V0, 0, pl.ds(16, 16)] = value.astype(BF16)
        elif u < M0:
            qn[u - Q0] = head_norm(value, 0)
        else:
            k, c = (u - M0) // 4, (u - M0) % 4
            agb[k, c, 0] = (0.5 * value * (1.0 + lax.erf(value * (0.5 ** 0.5)))).astype(BF16)
            ag_step(k, c, 0)

    def kv_step(c, s):
        if s > 0:
            kv_copy(c, s - 1).wait_recv()
        if s < 3:
            start(kv_copy(c, s))

    def attention():
        row = lax.broadcasted_iota(jnp.int32, (48, HD), 0)
        first = (row & 15) * 24 + drow * 3 + (row >> 4) < c0
        queries = qn[...].reshape(48, 384)
        for h in range(3):
            cut = slice(h * HD, (h + 1) * HD)
            found = []
            for image in range(2):
                held = kv[pl.ds(2 * image, 2), :, :, cut]
                keys = held[:, :, 0:16].reshape(256, HD)
                values = held[:, :, 16:32].reshape(256, HD)
                scores = dot_t(queries[:, cut], keys) * HD ** (-0.5)
                expo = jnp.exp(scores - jnp.max(scores, -1, keepdims=True))
                weights = (expo / jnp.sum(expo, -1, keepdims=True)).astype(BF16)
                found.append(dot(weights, values))
            attended = jnp.where(first, found[0], found[1]).astype(BF16)
            for k in range(3):
                agb[k, 4, 0, :, cut] = attended[k * 16:(k + 1) * 16]
        for k in range(3):
            ag_step(k, 4, 0)

    begun, loaded_wd = set(), set()

    def branch(k, i):
        ag_step(k, i, 4)
        c = i if i < 4 else A_CLASS[k]
        value = None
        for h in range(2):
            left = jnp.concatenate([agb[k, i, place_of(c, b, h)] for b in range(8)], axis=0)
            if (i, h) not in loaded_wd:
                load_wd[i, h].wait()
                loaded_wd.add((i, h))
            part = dot(left, wd[i, h])
            value = part if value is None else value + part
        value = value.reshape(8, 16, 384)
        bsum[k] = bsum[k] + value if k in begun else value
        begun.add(k)

    def z_send(k):
        zs[k] = bsum[k].astype(BF16)
        for o in range(7):
            src = zs.at[k, relative(column[o])]
            start(remote(src, zr.at[k, o], z_s.at[k, o], z_r.at[k], (dp, mx, column[o])))

    def adapt(k):
        if not begun & {"a"}:
            adapter_ready()
            begun.add("a")
        remote(zr.at[k], zr.at[k], z_s.at[k, 0], z_r.at[k], (dp, mx, column[0])).wait_recv()
        value = bsum[k, relative(z)]
        for o in range(7):
            value = value + zr[k, o].astype(F32)
        updated = (xz[pl.ds(k * 16, 16)] + value).astype(BF16)
        for b in range(8):
            part = dot(updated, wa[b])
            for j in range(4):
                tr[k, pl.ds(b * 4 + j, 16, stride=32), :] = part[:, j * 128:(j + 1) * 128]
        fs[k] = tr[k].astype(BF16).reshape(16, 32, 128)
        for o in range(15):
            start(remote(fs.at[k, plane[o]], fr.at[k, o], f_s.at[k, o], f_r.at[k], (dp, plane[o], z)))

    def finish(k):
        remote(fr.at[k], fr.at[k], f_s.at[k, 0], f_r.at[k], (dp, plane[0], z)).wait_recv()
        value = tr[k, pl.ds(pl.multiple_of(mx * 32, 32), 32)]
        for o in range(15):
            value = value + fr[k, o].astype(F32)
        out_ref[k] = value.astype(BF16)

    def adapter_ready():
        load_wa.wait()
        for way in range(2):
            for s in range(1, 5 - way):
                across_copy(way, s).wait_recv()

    def residual():
        row = lax.broadcasted_iota(jnp.int32, (48, 128), 0)
        xz[...] = dot(pick((row & 15) * 24 + z * 3 + (row >> 4)), xb)

    def drain():
        while sent:
            sent.pop(0).wait_send()

    def greet():
        pl.semaphore_wait(barrier, 7)

    events = {
        "greet": greet, "p": product, "r": rs_step, "e": rs_end, "v": kv_step, "att": attention, "g": ag_step,
        "b": branch, "z": z_send, "a": adapt, "f": finish, "w": ring_step, "s": stat_step, "c": c_step,
        "n": correct, "d": drain, "x": residual, "ch": choose,
    }
    for event in ORDER:
        events[event[0]](*event[1:])
    drain()


def per_device(patches, ln_gain, w_qkv, qk_gain, w_out, w_up, w_down, w_adapt, patch_counts):
    vmem, hbm = pl.BlockSpec(memory_space=pltpu.VMEM), pl.BlockSpec(memory_space=pl.ANY)
    dma = pltpu.SemaphoreType.DMA
    out = pl.pallas_call(
        kernel,
        out_shape=jax.ShapeDtypeStruct((3, 32, 128), BF16),
        in_specs=[hbm, vmem, hbm, vmem, hbm, hbm, hbm, hbm, pl.BlockSpec(memory_space=pltpu.SMEM)],
        out_specs=vmem,
        scratch_shapes=[
            pltpu.VMEM((512, 384), BF16),
            pltpu.VMEM((7, 8, 16, 384), BF16),
            pltpu.VMEM((7, 2, 384, 384), BF16),
            pltpu.VMEM((5, 2, 384, 384), BF16),
            pltpu.VMEM((8, 384, 512), BF16),
            pltpu.VMEM((16, 2, 512), F32),
            pltpu.VMEM((16, 384), BF16),
            pltpu.VMEM((16, 16, 384), BF16),
            pltpu.VMEM((4, 8, 16, 128), BF16),
            pltpu.VMEM((UNITS, 16, 384), F32),
            pltpu.VMEM((UNITS, 16, 128), F32),
            pltpu.VMEM((UNITS, 8, 16, 384), F32),
            pltpu.VMEM((UNITS, 15, 16, 384), BF16),
            pltpu.VMEM((UNITS, 15, 16, 384), BF16),
            pltpu.VMEM((4, 8, 32, 384), BF16),
            pltpu.VMEM((3, 16, 384), BF16),
            pltpu.VMEM((3, 5, 16, 16, 384), BF16),
            pltpu.VMEM((3, 8, 16, 384), BF16),
            pltpu.VMEM((3, 8, 16, 384), F32),
            pltpu.VMEM((3, 7, 16, 384), BF16),
            pltpu.VMEM((48, 384), F32),
            pltpu.VMEM((3, 512, 128), F32),
            pltpu.VMEM((3, 16, 32, 128), BF16),
            pltpu.VMEM((3, 15, 32, 128), BF16),
            dma, dma((7, 2)), dma((5, 2)), dma,
            dma((4,)), dma((4,)),
            dma((4,)), dma((4,)),
            dma((UNITS, 4)), dma((UNITS, 4)),
            dma((4, 3)), dma((4, 3)),
            dma((3, 5, 4)), dma((3, 5, 4)),
            dma((3, 7)), dma((3,)),
            dma((3, 15)), dma((3,)),
            dma((7,)), dma((7,)),
            dma((7,)), dma((7,)),
        ],
        compiler_params=pltpu.CompilerParams(
            collective_id=0, has_side_effects=True, vmem_limit_bytes=60 * 2**20
        ),
    )(patches, ln_gain.reshape(1, 384), w_qkv, qk_gain, w_out, w_up, w_down, w_adapt, patch_counts)
    return out.reshape(3, 4096)


def solution(mesh):
    return jax.shard_map(
        per_device,
        mesh=mesh,
        in_specs=(
            P("dp", "mx"),
            P("mx"),
            P(None, "mx", "my"),
            P(None, "my"),
            P("my", "mx"),
            P("mx", "my"),
            P("my", "mx"),
            P("mx", "my"),
            P("dp", None),
        ),
        out_specs=P(("dp", "mx", "my"), None),
        check_vma=False,
    )
```

```python
import jax
import jax.numpy as jnp
from jax import lax
from jax.experimental import pallas as pl
from jax.experimental.pallas import tpu as pltpu
from jax.sharding import PartitionSpec as P

MESH = pl.DeviceIdType.MESH
D = 6144
HD = 128
F32 = jnp.float32
BF16 = jnp.bfloat16

Q0, M0, UNITS = 4, 7, 19
Q_CLASS, A_CLASS = (3, 0, 2), (3, 1, 2)
CLASS = (0, 1, 2, 3) + Q_CLASS + (0, 1, 2, 3) * 3
BLOCKS = (
    [(c, 1) for c in range(4)]
    + [(c, 2) for c in range(4)]
    + [(4 + k, 0) for k in range(3)]
    + [(4 + k, 3 + c) for k in range(3) for c in range(4)]
)
KV_LINKS = ((0, 1, 2), (1, 2, 0), (2, 0, 1), (2, 1, 0))
FIRST = (3, 0, 1, 2)

ORDER = (
    ("ch",), ("x",), ("greet",), ("p", 18), ("p", 17), ("p", 16), ("p", 0), ("s", 0), ("p", 10), ("p", 12), ("p", 13),
    ("c", 0), ("p", 2), ("p", 1), ("p", 7), ("p", 14), ("w", 0), ("r", 17, 1), ("r", 16, 1), ("s", 1), ("r", 18, 1),
    ("p", 3), ("c", 1), ("r", 10, 1), ("r", 12, 1), ("r", 13, 1), ("r", 0, 1), ("p", 11), ("r", 14, 1), ("r", 7, 1),
    ("p", 9), ("s", 2), ("r", 17, 2), ("r", 18, 2), ("r", 2, 1), ("r", 1, 1), ("c", 2), ("w", 1), ("r", 16, 2),
    ("r", 10, 2), ("p", 15), ("r", 12, 2), ("p", 8), ("r", 0, 2), ("r", 3, 1), ("r", 7, 2), ("r", 11, 1), ("s", 3),
    ("r", 9, 1), ("r", 18, 3), ("r", 13, 2), ("r", 14, 2), ("r", 17, 3), ("c", 3), ("r", 10, 3), ("p", 4), ("p", 5),
    ("r", 1, 2), ("r", 16, 3), ("r", 15, 1), ("r", 2, 2), ("p", 6), ("r", 8, 1), ("r", 7, 3), ("r", 12, 3), ("w", 2),
    ("s", 4), ("r", 11, 2), ("r", 3, 2), ("r", 9, 2), ("r", 14, 3), ("r", 13, 3), ("r", 15, 2), ("c", 4), ("n",),
    ("e", 18), ("e", 17), ("r", 4, 1), ("e", 0), ("e", 1), ("e", 16), ("e", 13), ("e", 7), ("e", 2), ("r", 8, 2),
    ("r", 11, 3), ("r", 9, 3), ("e", 12), ("g", 2, 2, 1), ("e", 10), ("r", 5, 1), ("e", 3), ("e", 14), ("r", 15, 3),
    ("g", 0, 0, 1), ("g", 2, 3, 1), ("v", 0, 1), ("g", 2, 1, 1), ("g", 1, 2, 1), ("r", 6, 1), ("r", 4, 2),
    ("r", 8, 3), ("e", 11), ("v", 1, 1), ("g", 1, 1, 1), ("e", 9), ("w", 3), ("g", 2, 2, 2), ("v", 2, 1), ("r", 5, 2),
    ("e", 15), ("g", 0, 3, 1), ("g", 2, 1, 2), ("v", 3, 1), ("g", 1, 2, 2), ("g", 1, 3, 1), ("e", 8), ("g", 2, 3, 2),
    ("g", 0, 0, 2), ("r", 6, 2), ("g", 1, 0, 1), ("g", 0, 2, 1), ("g", 1, 1, 2), ("v", 1, 2), ("g", 2, 2, 3),
    ("v", 0, 2), ("e", 4), ("v", 2, 2), ("g", 2, 0, 1), ("e", 5), ("g", 0, 3, 2), ("g", 1, 3, 2), ("g", 1, 2, 3),
    ("v", 3, 2), ("g", 2, 1, 3), ("g", 0, 1, 1), ("w", 4), ("g", 1, 0, 2), ("g", 0, 0, 3), ("g", 2, 3, 3),
    ("g", 1, 1, 3), ("e", 6), ("att",), ("g", 0, 2, 2), ("g", 2, 0, 2), ("g", 0, 1, 2), ("g", 1, 3, 3), ("b", 2, 1),
    ("g", 0, 3, 3), ("b", 2, 2), ("g", 1, 0, 3), ("b", 2, 3), ("b", 0, 0), ("b", 1, 2), ("g", 1, 4, 1), ("b", 1, 1),
    ("g", 0, 2, 3), ("g", 0, 4, 1), ("g", 0, 1, 3), ("g", 2, 4, 1), ("g", 2, 0, 3), ("b", 1, 3), ("b", 1, 0),
    ("b", 1, 4), ("z", 1), ("b", 0, 3), ("b", 0, 2), ("b", 0, 1), ("b", 0, 4), ("z", 0), ("b", 2, 0), ("b", 2, 4),
    ("z", 2), ("a", 1), ("a", 0), ("d",), ("a", 2), ("f", 1), ("f", 0), ("f", 2),
)


def dot(a, b):
    return jnp.dot(a, b, preferred_element_type=F32)


def dot_t(a, b):
    return lax.dot_general(a, b, (((1,), (1,)), ((), ())), preferred_element_type=F32)


def kernel(
    x_hbm, gain_ref, wqkv_hbm, qkg_ref, wout_hbm, wup_hbm, wdown_hbm, wad_hbm, cnt_ref,
    out_ref,
    x, a, wv, wd, wa, stat, cpk, cr, tt, corr, rst, acc, snd, rcv, acc2, snd2, rcv2, kv, qn, agb, zs, bsum, zr, xz, tr, fs, fr,
    sem_x, sem_wv, sem_wd, sem_wa,
    stat_s, stat_r, c_s, c_r, rs_s, rs_r, kv_s, kv_r, ag_s, ag_r, z_s, z_r, f_s, f_r, wz_s, wz_r, wc_s, wc_r,
):
    dp, mx, z = lax.axis_index("dp"), lax.axis_index("mx"), lax.axis_index("my")
    cy, cx = mx // 4, mx % 4
    vx, vy = cx // 2, cy // 2
    ux = cx % 2 + vx - 2 * (cx % 2) * vx
    uy = cy % 2 + vy - 2 * (cy % 2) * vy
    bits = (ux, uy, vx, vy)
    drow = ux * 4 + uy * 2 + vx
    halves = (vy, 1 - vy)

    def flip(c):
        return c + 1 - 2 * (c % 2)

    def towards(*dims):
        py, px = cy, cx
        for d in dims:
            if d == 0:
                px = flip(px)
            elif d == 1:
                py = flip(py)
            elif d == 2:
                px = 3 - px
            else:
                py = 3 - py
        return (dp, py * 4 + px, z)

    partners = tuple(towards(d) for d in range(4))
    plane = [((cy + o // 4) % 4) * 4 + (cx + o % 4) % 4 for o in range(1, 16)]
    column = [(z + o) % 8 for o in range(1, 8)]
    other = (1 - dp, mx, z)

    def relative(block):
        total = 0
        for bit, weight in ((block // 4, 4), ((block // 2) % 2, 2), (block % 2, 1)):
            own = bits[{4: 0, 2: 1, 1: 2}[weight]]
            total = total + weight * (bit + own - 2 * bit * own)
        return total

    sent = []

    def remote(src, dst, s, r, device):
        return pltpu.make_async_remote_copy(
            src_ref=src, dst_ref=dst, send_sem=s, recv_sem=r, device_id=device, device_id_type=MESH
        )

    def start(copy):
        copy.start()
        sent.append(copy)

    barrier = pltpu.get_barrier_semaphore()
    for device in partners + ((dp, mx, column[0]), (dp, mx, column[6]), other):
        pl.semaphore_signal(barrier, inc=1, device_id=device, device_id_type=MESH)

    load_x = pltpu.make_async_copy(x_hbm, x, sem_x)
    load_x.start()
    load_wv, load_wd = {}, {}

    def half_at(base, half):
        return pl.ds(pl.multiple_of(base + half * 384, 128), 384)

    for i in (1, 2, 0, 3, 4, 5, 6):
        for h in range(2):
            if i < 3:
                src = wqkv_hbm.at[i, :, half_at(0, halves[h])]
            else:
                src = wup_hbm.at[:, half_at((i - 3) * 768, halves[h])]
            load_wv[i, h] = pltpu.make_async_copy(src, wv.at[i, h], sem_wv.at[i, h])
            load_wv[i, h].start()
    load_wa = pltpu.make_async_copy(wad_hbm, wa.at[z], sem_wa)
    load_wa.start()
    for i in range(5):
        for h in range(2):
            src = wdown_hbm.at[half_at(i * 768, halves[h])] if i < 4 else wout_hbm.at[half_at(0, halves[h])]
            load_wd[i, h] = pltpu.make_async_copy(src, wd.at[i, h], sem_wd.at[i, h])
            load_wd[i, h].start()

    mine = pl.ds(pl.multiple_of(dp * 192, 16), 192)

    def ring_copy(way, s):
        block, to = ((z + 8 - s) % 8, (z + 1) % 8) if way == 0 else ((z + s) % 8, (z + 7) % 8)
        i = way * 4 + s
        return remote(wa.at[block, mine], wa.at[block, mine], wz_s.at[i], wz_r.at[i], (dp, mx, to))

    def across_copy(way, s):
        block = (z + 8 - s) % 8 if way == 0 else (z + s) % 8
        i = way * 4 + s - 1
        return remote(wa.at[block, mine], wa.at[block, mine], wc_s.at[i], wc_r.at[i], other)

    def ring_step(s):
        if s == 0:
            load_wa.wait()
        for way in range(2):
            steps = 4 - way
            if 0 < s <= steps:
                ring_copy(way, s - 1).wait_recv()
            if s < steps:
                start(ring_copy(way, s))
            if 0 < s <= steps:
                start(across_copy(way, s))

    load_x.wait()
    xb = x[...]
    xf = xb.astype(F32)
    gain = gain_ref[...]
    centred = ((xf - jnp.mean(xf, -1, keepdims=True)) * gain).astype(BF16)
    for b in range(8):
        place = relative(b)
        for g in range(4):
            a[g, place] = centred[g * 128 + b * 16:g * 128 + b * 16 + 16]

    c0 = cnt_ref[0, 0]

    def pick(slot):
        token = slot + jnp.where(slot >= c0, 256 - c0, 0)
        lane = lax.broadcasted_iota(jnp.int32, token.shape, 1)
        return jnp.concatenate([jnp.where(token == lane + 128 * j, 1.0, 0.0).astype(BF16) for j in range(4)], axis=1)

    def choose():
        row = lax.broadcasted_iota(jnp.int32, (384, 128), 0)
        block = jnp.bitwise_xor((row >> 4) & 7, drow)
        chosen = pick((row & 15) * 24 + block * 3 + (row >> 7))
        for k in range(3):
            a[4 + k] = dot(chosen[k * 128:(k + 1) * 128], centred).astype(BF16).reshape(8, 16, 384)

    loaded = set()

    def weights(w, h):
        if (w, h) not in loaded:
            load_wv[w, h].wait()
            loaded.add((w, h))
        return wv[w, h]

    def stat_copy(s):
        n = 1 << s
        return remote(stat.at[pl.ds(0, n)], stat.at[pl.ds(n, n)], stat_s.at[s], stat_r.at[s], partners[FIRST[s]])

    def stat_step(s):
        if s == 0:
            row8 = lax.broadcasted_iota(jnp.int32, (8, 384), 0)
            e0, e1 = (row8 == 0).astype(F32).astype(BF16), (row8 == 1).astype(F32).astype(BF16)
            x2 = xf * xf
            hi = x2.astype(BF16)
            lo = (x2 - hi.astype(F32)).astype(BF16)
            stat[0] = (dot_t(e0, xb) + dot_t(e1, hi) + dot_t(e1, lo))[0:2]
        else:
            stat_copy(s - 1).wait_recv()
        if s < 4:
            start(stat_copy(s))

    def split(value):
        hi = value.astype(BF16).astype(F32)
        return hi, (value - hi).astype(BF16).astype(F32)

    def c_copy(s):
        if s == 0:
            src, dst = cpk, cr.at[1]
        else:
            n = 1 << s
            src, dst = cr.at[pl.ds(0, n)], cr.at[pl.ds(n, n)]
        return remote(src, dst, c_s.at[s], c_r.at[s], partners[FIRST[s]])

    def c_step(s):
        if s == 0:
            g0, rest = split(gain)
            g1, g2 = split(gain - g0)
            row24 = lax.broadcasted_iota(jnp.int32, (24, 384), 0)
            parts = jnp.where(row24 < 8, g0, jnp.where(row24 < 16, g1, g2))
            for h in (1, 0):
                value = None
                for w in range(7):
                    left = jnp.where((row24 & 7) == w, parts, 0.0).astype(BF16)
                    part = dot(left, weights(w, h))
                    value = part if value is None else value + part
                sums = jnp.concatenate(split(value[0:8] + value[8:16] + value[16:24]), axis=0).astype(BF16)
                if h == 1:
                    cpk[...] = sums
                else:
                    cr[0] = sums
        else:
            c_copy(s - 1).wait_recv()
        if s < 4:
            start(c_copy(s))

    def correct():
        sums = jnp.concatenate([stat[j][0:1] for j in range(16)], axis=0)
        squares = jnp.concatenate([stat[j][1:2] for j in range(16)], axis=0)
        mean = jnp.sum(sums, 0, keepdims=True) * (1.0 / D)
        square = jnp.sum(squares, 0, keepdims=True) * (1.0 / D)
        scale = lax.rsqrt(square - mean * mean + 1e-06)
        hi, lo = split(sums * (1.0 / 384) - mean)
        s0, rest = split(scale)
        s1, s2 = split(scale - s0)
        row8 = lax.broadcasted_iota(jnp.int32, (8, 512), 0)
        scales = jnp.where(row8 == 0, s0, jnp.where(row8 == 1, s1, jnp.where(row8 == 2, s2, 0.0)))
        table = jnp.concatenate([hi, lo, scales, jnp.zeros((88, 512), F32)], axis=0)
        table = jnp.transpose(table).astype(BF16)
        tt[...] = table.reshape(4, 8, 16, 128)
        row = lax.broadcasted_iota(jnp.int32, (48, 128), 0)
        own = dot(pick((row & 15) * 24 + drow * 3 + (row >> 4)), table).astype(BF16)
        rows = [tt[r, drow] if r < 4 else own[(r - 4) * 16:(r - 3) * 16] for r, w in BLOCKS]
        left = jnp.concatenate(rows, axis=0)
        j = lax.broadcasted_iota(jnp.int32, (128, 256), 0)
        lane = lax.broadcasted_iota(jnp.int32, (128, 256), 1)
        spread_hi = jnp.where((lane >> 4) == j, 1.0, 0.0).astype(BF16)
        spread_lo = jnp.where((lane >> 4) + 16 == j, 1.0, 0.0).astype(BF16)
        j = lax.broadcasted_iota(jnp.int32, (128, 128), 0)
        spread_scale = jnp.where((j >= 32) & (j < 35), 1.0, 0.0).astype(BF16)
        rst[...] = dot(left, spread_scale).reshape(23, 16, 128)
        unit = lax.broadcasted_iota(jnp.int32, (368, 256), 0) >> 4
        group = jnp.where(unit < 4, 1, jnp.where(unit < 8, 2, jnp.where(unit < 11, 0, 3 + ((unit - 11) & 3))))
        at = lax.broadcasted_iota(jnp.int32, (368, 256), 1) & 15
        left_hi = jnp.where((at & 7) == group, dot(left, spread_hi), 0.0).astype(BF16)
        left_lo = jnp.where(at == group, dot(left, spread_lo), 0.0).astype(BF16)
        held = cr[...].reshape(256, 384)
        corr[...] = (dot(left_hi, held) + dot(left_lo, held)).reshape(23, 16, 384)

    def offset(t):
        return 16 - (16 >> t)

    def held_by(u):
        return (acc2.at[u], snd2.at[u], rcv2.at[u]) if u < Q0 else (acc.at[u - Q0], snd.at[u - Q0], rcv.at[u - Q0])

    def rs_copies(u, t):
        own, out, come = held_by(u)
        c = CLASS[u]
        if t < 2 or u >= M0:
            parts = [(pl.ds(offset(t), 8 >> t), t, ((c + t) % 4,))]
        else:
            d, e = (c + 2) % 4, (c + 3) % 4
            parts = [(12, 2, (e,)), (13, 3, (d,)), (14, 4, (d, e))]
        return [
            remote(out.at[at], come.at[at], rs_s.at[u, i], rs_r.at[u, i], towards(*dims)) for at, i, dims in parts
        ]

    def place_of(c, b, h):
        own = ((b >> 2) & 1, (b >> 1) & 1, b & 1, h)
        return sum(own[(c + t) % 4] << (3 - t) for t in range(4))

    def product(u):
        own, out, come = held_by(u)
        c = CLASS[u]
        if u < Q0:
            halves_of = [(a[u], 1, 0), (a[u], 2, 16)]
        elif u < M0:
            halves_of = [(a[u], 0, 0)]
        else:
            halves_of = [(a[4 + (u - M0) // 4], 3 + (u - M0) % 4, 0)]
        for left, w, first in halves_of:
            left = left.reshape(128, 384)
            for h in range(2):
                value = dot(left, weights(w, h))
                for b in range(8):
                    j = place_of(c, b, h)
                    part = value[b * 16:(b + 1) * 16]
                    if j >= 8:
                        out[j - 8, pl.ds(first, 16)] = part.astype(BF16)
                    else:
                        own[j, pl.ds(first, 16)] = part
        for copy in rs_copies(u, 0):
            start(copy)

    def rs_step(u, t):
        own, out, come = held_by(u)
        for copy in rs_copies(u, t - 1):
            copy.wait_recv()
        n, at, to = 8 >> (t - 1), offset(t - 1), offset(t)
        keep = 1 if t == 2 and u < M0 else n // 2
        out[pl.ds(to, n - keep)] = (
            own[pl.ds(keep, n - keep)] + come[pl.ds(at + keep, n - keep)].astype(F32)
        ).astype(BF16)
        for copy in rs_copies(u, t):
            start(copy)
        own[pl.ds(0, keep)] = own[pl.ds(0, keep)] + come[pl.ds(at, keep)].astype(F32)

    def rs_last(u):
        own, out, come = held_by(u)
        for copy in rs_copies(u, 2 if u < M0 else 3):
            copy.wait_recv()
        value = own[0]
        for i in range(12 if u < M0 else 14, 15):
            value = value + come[i].astype(F32)
        return value

    def corrected(value, block):
        return (value + corr[block]) * jnp.concatenate([rst[block]] * 3, axis=1)

    head_gain = qkg_ref[:, half_at(0, vy)]

    def head_norm(value, which):
        parts = []
        for h in range(3):
            cut = slice(h * HD, (h + 1) * HD)
            v = value[:, cut]
            mean = jnp.mean(v, -1, keepdims=True)
            square = jnp.mean(v * v, -1, keepdims=True)
            parts.append((v - mean) * lax.rsqrt(square - mean * mean + 1e-06) * head_gain[which:which + 1, cut])
        return jnp.concatenate(parts, axis=1).astype(BF16)

    def kv_copies(c, s):
        links = KV_LINKS[c]
        if s == 0:
            parts = [(0, 1, 0, links[:1]), (0, 2, 1, links[1:2]), (0, 3, 2, links[:2])]
        else:
            parts = [(pl.ds(0, 4), pl.ds(4, 4), 3, links[2:])]
        return [
            remote(kv.at[c, at], kv.at[c, to], kv_s.at[c, i], kv_r.at[c, i], towards(*dims)) for at, to, i, dims in parts
        ]

    def ag_copies(k, i, s):
        c = i if i < 4 else A_CLASS[k]
        if i < 4:
            n = 1 << s
            parts = [(pl.ds(0, n), pl.ds(n, n), s, ((c + 3 - s) % 4,))]
        else:
            n, d, e = 1 << 2 * s, (c + 3 - 2 * s) % 4, (c + 2 - 2 * s) % 4
            parts = [
                (pl.ds(0, n), pl.ds(n * m, n), 3 * s + m - 1, dims) for m, dims in ((1, (d,)), (2, (e,)), (3, (d, e)))
            ]
        return [
            remote(agb.at[k, i, at], agb.at[k, i, to], ag_s.at[k, i, j], ag_r.at[k, i, j], towards(*dims))
            for at, to, j, dims in parts
        ]

    def ag_step(k, i, s):
        if s > 0:
            for copy in ag_copies(k, i, s - 1):
                copy.wait_recv()
        if s < (4 if i < 4 else 2):
            for copy in ag_copies(k, i, s):
                start(copy)

    def rs_end(u):
        value = rs_last(u)
        if u < Q0:
            kv[u, 0, pl.ds(0, 16)] = head_norm(corrected(value[0:16], u), 1)
            kv[u, 0, pl.ds(16, 16)] = corrected(value[16:32], 4 + u).astype(BF16)
            kv_step(u, 0)
        elif u < M0:
            qn[u - Q0] = head_norm(corrected(value, 4 + u), 0)
        else:
            k, c = (u - M0) // 4, (u - M0) % 4
            value = corrected(value, 4 + u)
            agb[k, c, 0] = (0.5 * value * (1.0 + lax.erf(value * (0.5 ** 0.5)))).astype(BF16)
            ag_step(k, c, 0)

    def kv_step(c, s):
        if s > 0:
            for copy in kv_copies(c, s - 1):
                copy.wait_recv()
        if s < 2:
            for copy in kv_copies(c, s):
                start(copy)

    def attention():
        row = lax.broadcasted_iota(jnp.int32, (48, HD), 0)
        first = (row & 15) * 24 + drow * 3 + (row >> 4) < c0
        queries = qn[...].reshape(48, 384)
        for h in range(3):
            cut = slice(h * HD, (h + 1) * HD)
            found = []
            for image in range(2):
                held = kv[pl.ds(2 * image, 2), :, :, cut]
                keys = held[:, :, 0:16].reshape(256, HD)
                values = held[:, :, 16:32].reshape(256, HD)
                scores = dot_t(queries[:, cut], keys) * HD ** (-0.5)
                expo = jnp.exp(scores - jnp.max(scores, -1, keepdims=True))
                weights = (expo / jnp.sum(expo, -1, keepdims=True)).astype(BF16)
                found.append(dot(weights, values))
            attended = jnp.where(first, found[0], found[1]).astype(BF16)
            for k in range(3):
                agb[k, 4, 0, :, cut] = attended[k * 16:(k + 1) * 16]
        for k in range(3):
            ag_step(k, 4, 0)

    begun, loaded_wd = set(), set()

    def branch(k, i):
        ag_step(k, i, 4 if i < 4 else 2)
        c = i if i < 4 else A_CLASS[k]
        value = None
        for h in range(2):
            left = jnp.concatenate([agb[k, i, place_of(c, b, h)] for b in range(8)], axis=0)
            if (i, h) not in loaded_wd:
                load_wd[i, h].wait()
                loaded_wd.add((i, h))
            part = dot(left, wd[i, h])
            value = part if value is None else value + part
        value = value.reshape(8, 16, 384)
        bsum[k] = bsum[k] + value if k in begun else value
        begun.add(k)

    def z_send(k):
        zs[k] = bsum[k].astype(BF16)
        for o in range(7):
            src = zs.at[k, relative(column[o])]
            start(remote(src, zr.at[k, o], z_s.at[k, o], z_r.at[k], (dp, mx, column[o])))

    def adapt(k):
        if not begun & {"a"}:
            adapter_ready()
            begun.add("a")
        remote(zr.at[k], zr.at[k], z_s.at[k, 0], z_r.at[k], (dp, mx, column[0])).wait_recv()
        value = bsum[k, relative(z)]
        for o in range(7):
            value = value + zr[k, o].astype(F32)
        updated = (xz[pl.ds(k * 16, 16)] + value).astype(BF16)
        for b in range(8):
            part = dot(updated, wa[b])
            for j in range(4):
                tr[k, pl.ds(b * 4 + j, 16, stride=32), :] = part[:, j * 128:(j + 1) * 128]
        fs[k] = tr[k].astype(BF16).reshape(16, 32, 128)
        for o in range(15):
            start(remote(fs.at[k, plane[o]], fr.at[k, o], f_s.at[k, o], f_r.at[k], (dp, plane[o], z)))

    def finish(k):
        remote(fr.at[k], fr.at[k], f_s.at[k, 0], f_r.at[k], (dp, plane[0], z)).wait_recv()
        value = tr[k, pl.ds(pl.multiple_of(mx * 32, 32), 32)]
        for o in range(15):
            value = value + fr[k, o].astype(F32)
        out_ref[k] = value.astype(BF16)

    def adapter_ready():
        for way in range(2):
            for s in range(1, 5 - way):
                across_copy(way, s).wait_recv()

    def residual():
        row = lax.broadcasted_iota(jnp.int32, (48, 128), 0)
        xz[...] = dot(pick((row & 15) * 24 + z * 3 + (row >> 4)), xb)

    def drain():
        while sent:
            sent.pop(0).wait_send()

    def greet():
        pl.semaphore_wait(barrier, 7)

    events = {
        "greet": greet, "p": product, "r": rs_step, "e": rs_end, "v": kv_step, "att": attention, "g": ag_step,
        "b": branch, "z": z_send, "a": adapt, "f": finish, "w": ring_step, "s": stat_step, "c": c_step,
        "n": correct, "d": drain, "x": residual, "ch": choose,
    }
    for event in ORDER:
        events[event[0]](*event[1:])
    drain()


def per_device(patches, ln_gain, w_qkv, qk_gain, w_out, w_up, w_down, w_adapt, patch_counts):
    vmem, hbm = pl.BlockSpec(memory_space=pltpu.VMEM), pl.BlockSpec(memory_space=pl.ANY)
    dma = pltpu.SemaphoreType.DMA
    out = pl.pallas_call(
        kernel,
        out_shape=jax.ShapeDtypeStruct((3, 32, 128), BF16),
        in_specs=[hbm, vmem, hbm, vmem, hbm, hbm, hbm, hbm, pl.BlockSpec(memory_space=pltpu.SMEM)],
        out_specs=vmem,
        scratch_shapes=[
            pltpu.VMEM((512, 384), BF16),
            pltpu.VMEM((7, 8, 16, 384), BF16),
            pltpu.VMEM((7, 2, 384, 384), BF16),
            pltpu.VMEM((5, 2, 384, 384), BF16),
            pltpu.VMEM((8, 384, 512), BF16),
            pltpu.VMEM((16, 2, 512), F32),
            pltpu.VMEM((16, 384), BF16),
            pltpu.VMEM((16, 16, 384), BF16),
            pltpu.VMEM((4, 8, 16, 128), BF16),
            pltpu.VMEM((23, 16, 384), F32),
            pltpu.VMEM((23, 16, 128), F32),
            pltpu.VMEM((UNITS - Q0, 8, 16, 384), F32),
            pltpu.VMEM((UNITS - Q0, 15, 16, 384), BF16),
            pltpu.VMEM((UNITS - Q0, 15, 16, 384), BF16),
            pltpu.VMEM((Q0, 8, 32, 384), F32),
            pltpu.VMEM((Q0, 15, 32, 384), BF16),
            pltpu.VMEM((Q0, 15, 32, 384), BF16),
            pltpu.VMEM((4, 8, 32, 384), BF16),
            pltpu.VMEM((3, 16, 384), BF16),
            pltpu.VMEM((3, 5, 16, 16, 384), BF16),
            pltpu.VMEM((3, 8, 16, 384), BF16),
            pltpu.VMEM((3, 8, 16, 384), F32),
            pltpu.VMEM((3, 7, 16, 384), BF16),
            pltpu.VMEM((48, 384), F32),
            pltpu.VMEM((3, 512, 128), F32),
            pltpu.VMEM((3, 16, 32, 128), BF16),
            pltpu.VMEM((3, 15, 32, 128), BF16),
            dma, dma((7, 2)), dma((5, 2)), dma,
            dma((4,)), dma((4,)),
            dma((4,)), dma((4,)),
            dma((UNITS, 5)), dma((UNITS, 5)),
            dma((4, 4)), dma((4, 4)),
            dma((3, 5, 6)), dma((3, 5, 6)),
            dma((3, 7)), dma((3,)),
            dma((3, 15)), dma((3,)),
            dma((7,)), dma((7,)),
            dma((7,)), dma((7,)),
        ],
        compiler_params=pltpu.CompilerParams(
            collective_id=0, has_side_effects=True, vmem_limit_bytes=60 * 2**20
        ),
    )(patches, ln_gain.reshape(1, 384), w_qkv, qk_gain, w_out, w_up, w_down, w_adapt, patch_counts)
    return out.reshape(3, 4096)


def solution(mesh):
    return jax.shard_map(
        per_device,
        mesh=mesh,
        in_specs=(
            P("dp", "mx"),
            P("mx"),
            P(None, "mx", "my"),
            P(None, "my"),
            P("my", "mx"),
            P("mx", "my"),
            P("my", "mx"),
            P("mx", "my"),
            P("dp", None),
        ),
        out_specs=P(("dp", "mx", "my"), None),
        check_vma=False,
    )
```

```python
import jax
import jax.numpy as jnp
from jax import lax
from jax.experimental import pallas as pl
from jax.experimental.pallas import tpu as pltpu
from jax.sharding import PartitionSpec as P

MESH = pl.DeviceIdType.MESH
D = 6144
HD = 128
F32 = jnp.float32
BF16 = jnp.bfloat16

Q0, M0, UNITS = 4, 7, 19
Q_CLASS, A_CLASS = (0, 2, 3), (0, 2, 3)
CLASS = (0, 1, 2, 3) + Q_CLASS + (0, 1, 2, 3) * 3
BLOCKS = (
    [(c, 1) for c in range(4)]
    + [(c, 2) for c in range(4)]
    + [(4 + k, 0) for k in range(3)]
    + [(4 + k, 3 + c) for k in range(3) for c in range(4)]
)
KV_LINKS = ((0, 1, 2), (1, 2, 0), (2, 0, 1), (2, 0, 1))
FIRST = (3, 0, 1, 2)

ORDER = (
    ("ch",), ("greet",), ("p", 9), ("p", 12), ("p", 14), ("p", 11), ("p", 10), ("p", 7), ("p", 17), ("p", 0),
    ("s", 0), ("p", 13), ("p", 16), ("p", 2), ("p", 1), ("p", 3), ("r", 12, 1), ("r", 11, 1), ("r", 14, 1), ("w", 0),
    ("r", 9, 1), ("p", 5), ("c", 0), ("r", 7, 1), ("p", 8), ("p", 18), ("p", 15), ("r", 13, 1), ("r", 16, 1),
    ("p", 6), ("r", 11, 2), ("r", 0, 1), ("r", 17, 1), ("r", 3, 1), ("r", 10, 1), ("s", 1), ("r", 12, 2), ("r", 9, 2),
    ("r", 14, 2), ("c", 1), ("r", 15, 1), ("r", 2, 1), ("r", 1, 1), ("r", 13, 2), ("r", 18, 1), ("r", 6, 1),
    ("r", 11, 3), ("r", 9, 3), ("r", 17, 2), ("r", 10, 2), ("r", 5, 1), ("r", 7, 2), ("r", 13, 3), ("p", 4),
    ("r", 14, 3), ("r", 12, 3), ("r", 3, 2), ("r", 0, 2), ("s", 2), ("r", 16, 2), ("r", 8, 1), ("r", 18, 2), ("c", 2),
    ("n",), ("w", 1), ("r", 2, 2), ("r", 10, 3), ("r", 17, 3), ("r", 15, 2), ("e", 13), ("e", 14), ("e", 11),
    ("r", 5, 2), ("r", 6, 2), ("r", 1, 2), ("e", 3), ("r", 4, 1), ("r", 18, 3), ("e", 9), ("e", 12), ("r", 16, 3),
    ("r", 7, 3), ("e", 17), ("e", 0), ("g", 1, 0, 1), ("r", 8, 2), ("e", 10), ("e", 2), ("r", 15, 3), ("e", 5),
    ("g", 1, 3, 1), ("e", 1), ("g", 1, 2, 1), ("w", 2), ("g", 0, 2, 1), ("e", 7), ("v", 3, 1), ("x",), ("g", 1, 1, 1),
    ("e", 16), ("e", 18), ("r", 4, 2), ("r", 8, 3), ("e", 15), ("g", 2, 2, 1), ("v", 0, 1), ("g", 1, 3, 2),
    ("g", 1, 0, 2), ("g", 1, 2, 2), ("g", 0, 3, 1), ("v", 2, 1), ("g", 0, 0, 1), ("v", 1, 1), ("g", 2, 1, 1),
    ("g", 1, 1, 2), ("g", 0, 2, 2), ("e", 8), ("e", 6), ("g", 2, 2, 2), ("w", 3), ("g", 2, 0, 1), ("g", 1, 3, 3),
    ("v", 3, 2), ("g", 2, 3, 1), ("g", 1, 2, 3), ("v", 0, 2), ("e", 4), ("g", 0, 0, 2), ("g", 0, 3, 2),
    ("g", 2, 1, 2), ("g", 1, 0, 3), ("g", 1, 1, 3), ("g", 0, 1, 1), ("v", 1, 2), ("v", 2, 2), ("att",),
    ("g", 2, 3, 2), ("g", 2, 0, 2), ("g", 0, 3, 3), ("g", 0, 0, 3), ("g", 0, 1, 2), ("g", 1, 4, 1), ("g", 0, 4, 1),
    ("g", 2, 3, 3), ("g", 2, 4, 1), ("g", 0, 2, 3), ("b", 1, 2), ("g", 2, 0, 3), ("b", 1, 3), ("g", 0, 1, 3),
    ("g", 2, 2, 3), ("b", 1, 0), ("b", 0, 3), ("b", 1, 1), ("b", 0, 0), ("g", 2, 1, 3), ("b", 1, 4), ("z", 1),
    ("b", 0, 4), ("b", 0, 2), ("b", 0, 1), ("z", 0), ("b", 2, 3), ("w", 4), ("b", 2, 4), ("b", 2, 1), ("b", 2, 2),
    ("b", 2, 0), ("z", 2), ("a", 1), ("a", 0), ("d",), ("a", 2), ("f", 1), ("f", 0), ("f", 2),
)


def dot(a, b):
    return jnp.dot(a, b, preferred_element_type=F32)


def dot_t(a, b):
    return lax.dot_general(a, b, (((1,), (1,)), ((), ())), preferred_element_type=F32)


def kernel(
    x_hbm, gain_ref, wqkv_hbm, qkg_ref, wout_hbm, wup_hbm, wdown_hbm, wad_hbm, cnt_ref,
    out_ref,
    x, a, wv, wd, wa, stat, cpk, cr, tt, corr, rst, acc, snd, rcv, acc2, snd2, rcv2, kv, qn, agb, zs, bsum, zr, xz, tr, fs, fr, res,
    sem_x, sem_wv, sem_wd, sem_wa,
    stat_s, stat_r, c_s, c_r, rs_s, rs_r, kv_s, kv_r, ag_s, ag_r, z_s, z_r, f_s, f_r, wz_s, wz_r, wc_s, wc_r,
):
    dp, mx, z = lax.axis_index("dp"), lax.axis_index("mx"), lax.axis_index("my")
    cy, cx = mx // 4, mx % 4
    vx, vy = cx // 2, cy // 2
    ux = cx % 2 + vx - 2 * (cx % 2) * vx
    uy = cy % 2 + vy - 2 * (cy % 2) * vy
    bits = (ux, uy, vx, vy)
    drow = ux * 4 + uy * 2 + vx
    halves = (vy, 1 - vy)

    def flip(c):
        return c + 1 - 2 * (c % 2)

    def towards(*dims):
        py, px = cy, cx
        for d in dims:
            if d == 0:
                px = flip(px)
            elif d == 1:
                py = flip(py)
            elif d == 2:
                px = 3 - px
            else:
                py = 3 - py
        return (dp, py * 4 + px, z)

    partners = tuple(towards(d) for d in range(4))
    plane = [((cy + o // 4) % 4) * 4 + (cx + o % 4) % 4 for o in range(1, 16)]
    column = [(z + o) % 8 for o in range(1, 8)]
    other = (1 - dp, mx, z)

    def relative(block):
        total = 0
        for bit, weight in ((block // 4, 4), ((block // 2) % 2, 2), (block % 2, 1)):
            own = bits[{4: 0, 2: 1, 1: 2}[weight]]
            total = total + weight * (bit + own - 2 * bit * own)
        return total

    sent = []

    def remote(src, dst, s, r, device):
        return pltpu.make_async_remote_copy(
            src_ref=src, dst_ref=dst, send_sem=s, recv_sem=r, device_id=device, device_id_type=MESH
        )

    def start(copy):
        copy.start()
        sent.append(copy)

    barrier = pltpu.get_barrier_semaphore()
    greeted = partners + (towards(*FIRST[:2]), towards(*FIRST[2:]), (dp, mx, column[0]), (dp, mx, column[6]), other)
    for device in greeted:
        pl.semaphore_signal(barrier, inc=1, device_id=device, device_id_type=MESH)

    load_x = pltpu.make_async_copy(x_hbm, x, sem_x)
    load_x.start()
    load_wv, load_wd = {}, {}

    def half_at(base, half):
        return pl.ds(pl.multiple_of(base + half * 384, 128), 384)

    for i in (1, 2, 0, 3, 4, 5, 6):
        for h in range(2):
            if i < 3:
                src = wqkv_hbm.at[i, :, half_at(0, halves[h])]
            else:
                src = wup_hbm.at[:, half_at((i - 3) * 768, halves[h])]
            load_wv[i, h] = pltpu.make_async_copy(src, wv.at[i, h], sem_wv.at[i, h])
            load_wv[i, h].start()
    load_wa = pltpu.make_async_copy(wad_hbm, wa.at[z], sem_wa)
    load_wa.start()
    for i in range(5):
        for h in range(2):
            src = wdown_hbm.at[half_at(i * 768, halves[h])] if i < 4 else wout_hbm.at[half_at(0, halves[h])]
            load_wd[i, h] = pltpu.make_async_copy(src, wd.at[i, h], sem_wd.at[i, h])
            load_wd[i, h].start()

    mine = pl.ds(pl.multiple_of(dp * 192, 16), 192)

    def ring_copy(way, s):
        block, to = ((z + 8 - s) % 8, (z + 1) % 8) if way == 0 else ((z + s) % 8, (z + 7) % 8)
        i = way * 4 + s
        return remote(wa.at[block, mine], wa.at[block, mine], wz_s.at[i], wz_r.at[i], (dp, mx, to))

    def across_copy(way, s):
        block = (z + 8 - s) % 8 if way == 0 else (z + s) % 8
        i = way * 4 + s - 1
        return remote(wa.at[block, mine], wa.at[block, mine], wc_s.at[i], wc_r.at[i], other)

    def ring_step(s):
        if s == 0:
            load_wa.wait()
        for way in range(2):
            steps = 4 - way
            if 0 < s <= steps:
                ring_copy(way, s - 1).wait_recv()
            if s < steps:
                start(ring_copy(way, s))
            if 0 < s <= steps:
                start(across_copy(way, s))

    load_x.wait()
    xb = x[...]
    xf = xb.astype(F32)
    gain = gain_ref[...].reshape(1, 384)
    centred = ((xf - jnp.mean(xf, -1, keepdims=True)) * gain).astype(BF16)
    for b in range(8):
        place = relative(b)
        for g in range(4):
            a[g, place] = centred[g * 128 + b * 16:g * 128 + b * 16 + 16]

    c0 = cnt_ref[0, 0]

    def pick(slot):
        token = slot + jnp.where(slot >= c0, 256 - c0, 0)
        lane = lax.broadcasted_iota(jnp.int32, token.shape, 1)
        return jnp.concatenate([jnp.where(token == lane + 128 * j, 1.0, 0.0).astype(BF16) for j in range(4)], axis=1)

    def choose():
        row = lax.broadcasted_iota(jnp.int32, (384, 128), 0)
        block = jnp.bitwise_xor((row >> 4) & 7, drow)
        chosen = pick((row & 15) * 24 + block * 3 + (row >> 7))
        for k in range(3):
            a[4 + k] = dot(chosen[k * 128:(k + 1) * 128], centred).astype(BF16).reshape(8, 16, 384)

    loaded = set()

    def weights(w, h):
        if (w, h) not in loaded:
            load_wv[w, h].wait()
            loaded.add((w, h))
        return wv[w, h]

    def spread(s):
        n, d, e = 1 << 2 * s, FIRST[2 * s], FIRST[2 * s + 1]
        return [
            (pl.ds(0, n), pl.ds(n * m, n), 3 * s + m - 1, dims) for m, dims in ((1, (d,)), (2, (e,)), (3, (d, e)))
        ]

    def stat_copies(s):
        return [
            remote(stat.at[at], stat.at[to], stat_s.at[i], stat_r.at[i], towards(*dims)) for at, to, i, dims in spread(s)
        ]

    def stat_step(s):
        if s == 0:
            row8 = lax.broadcasted_iota(jnp.int32, (8, 384), 0)
            e0, e1 = (row8 == 0).astype(F32).astype(BF16), (row8 == 1).astype(F32).astype(BF16)
            x2 = xf * xf
            hi = x2.astype(BF16)
            lo = (x2 - hi.astype(F32)).astype(BF16)
            stat[0] = (dot_t(e0, xb) + dot_t(e1, hi) + dot_t(e1, lo))[0:2]
        else:
            for copy in stat_copies(s - 1):
                copy.wait_recv()
        if s < 2:
            for copy in stat_copies(s):
                start(copy)

    def split(value):
        hi = value.astype(BF16).astype(F32)
        return hi, (value - hi).astype(BF16).astype(F32)

    def c_copies(s):
        return [
            remote(
                cpk.at[pl.ds(0, 1)] if s == 0 and 3 in dims else cr.at[at], cr.at[to], c_s.at[i], c_r.at[i], towards(*dims)
            )
            for at, to, i, dims in spread(s)
        ]

    def c_step(s):
        if s == 0:
            g0, rest = split(gain)
            g1, g2 = split(gain - g0)
            row24 = lax.broadcasted_iota(jnp.int32, (24, 384), 0)
            parts = jnp.where(row24 < 8, g0, jnp.where(row24 < 16, g1, g2))
            for h in (1, 0):
                value = None
                for w in range(7):
                    left = jnp.where((row24 & 7) == w, parts, 0.0).astype(BF16)
                    part = dot(left, weights(w, h))
                    value = part if value is None else value + part
                sums = jnp.concatenate(split(value[0:8] + value[8:16] + value[16:24]), axis=0).astype(BF16)
                if h == 1:
                    cpk[0] = sums
                else:
                    cr[0] = sums
        else:
            for copy in c_copies(s - 1):
                copy.wait_recv()
        if s < 2:
            for copy in c_copies(s):
                start(copy)

    def correct():
        sums = jnp.concatenate([stat[j][0:1] for j in range(16)], axis=0)
        squares = jnp.concatenate([stat[j][1:2] for j in range(16)], axis=0)
        mean = jnp.sum(sums, 0, keepdims=True) * (1.0 / D)
        square = jnp.sum(squares, 0, keepdims=True) * (1.0 / D)
        scale = lax.rsqrt(square - mean * mean + 1e-06)
        hi, lo = split(sums * (1.0 / 384) - mean)
        s0, rest = split(scale)
        s1, s2 = split(scale - s0)
        row8 = lax.broadcasted_iota(jnp.int32, (8, 512), 0)
        scales = jnp.where(row8 == 0, s0, jnp.where(row8 == 1, s1, jnp.where(row8 == 2, s2, 0.0)))
        table = jnp.concatenate([hi, lo, scales, jnp.zeros((88, 512), F32)], axis=0)
        table = jnp.transpose(table).astype(BF16)
        tt[...] = table.reshape(4, 8, 16, 128)
        row = lax.broadcasted_iota(jnp.int32, (48, 128), 0)
        own = dot(pick((row & 15) * 24 + drow * 3 + (row >> 4)), table).astype(BF16)
        rows = [tt[r, drow] if r < 4 else own[(r - 4) * 16:(r - 3) * 16] for r, w in BLOCKS]
        left = jnp.concatenate(rows, axis=0)
        j = lax.broadcasted_iota(jnp.int32, (128, 256), 0)
        lane = lax.broadcasted_iota(jnp.int32, (128, 256), 1)
        spread_hi = jnp.where((lane >> 4) == j, 1.0, 0.0).astype(BF16)
        spread_lo = jnp.where((lane >> 4) + 16 == j, 1.0, 0.0).astype(BF16)
        j = lax.broadcasted_iota(jnp.int32, (128, 128), 0)
        spread_scale = jnp.where((j >= 32) & (j < 35), 1.0, 0.0).astype(BF16)
        rst[...] = dot(left, spread_scale).reshape(23, 16, 128)
        unit = lax.broadcasted_iota(jnp.int32, (368, 256), 0) >> 4
        group = jnp.where(unit < 4, 1, jnp.where(unit < 8, 2, jnp.where(unit < 11, 0, 3 + ((unit - 11) & 3))))
        at = lax.broadcasted_iota(jnp.int32, (368, 256), 1) & 15
        left_hi = jnp.where((at & 7) == group, dot(left, spread_hi), 0.0).astype(BF16)
        left_lo = jnp.where(at == group, dot(left, spread_lo), 0.0).astype(BF16)
        held = cr[...].reshape(256, 384)
        corr[...] = (dot(left_hi, held) + dot(left_lo, held)).reshape(23, 16, 384)

    def offset(t):
        return 16 - (16 >> t)

    def held_by(u):
        return (acc2.at[u], snd2.at[u], rcv2.at[u]) if u < Q0 else (acc.at[u - Q0], snd.at[u - Q0], rcv.at[u - Q0])

    def rs_copies(u, t):
        own, out, come = held_by(u)
        c = CLASS[u]
        if t < 2 or u >= M0:
            parts = [(pl.ds(offset(t), 8 >> t), t, ((c + t) % 4,))]
        else:
            d, e = (c + 2) % 4, (c + 3) % 4
            parts = [(12, 2, (e,)), (13, 3, (d,)), (14, 4, (d, e))]
        return [
            remote(out.at[at], come.at[at], rs_s.at[u, i], rs_r.at[u, i], towards(*dims)) for at, i, dims in parts
        ]

    def place_of(c, b, h):
        own = ((b >> 2) & 1, (b >> 1) & 1, b & 1, h)
        return sum(own[(c + t) % 4] << (3 - t) for t in range(4))

    def product(u):
        own, out, come = held_by(u)
        c = CLASS[u]
        if u < Q0:
            halves_of = [(a[u], 1, 0), (a[u], 2, 16)]
        elif u < M0:
            halves_of = [(a[u], 0, 0)]
        else:
            halves_of = [(a[4 + (u - M0) // 4], 3 + (u - M0) % 4, 0)]
        for left, w, first in halves_of:
            left = left.reshape(128, 384)
            for h in range(2):
                value = dot(left, weights(w, h))
                for b in range(8):
                    j = place_of(c, b, h)
                    part = value[b * 16:(b + 1) * 16]
                    if j >= 8:
                        out[j - 8, pl.ds(first, 16)] = part.astype(BF16)
                    else:
                        own[j, pl.ds(first, 16)] = part
        for copy in rs_copies(u, 0):
            start(copy)

    def rs_step(u, t):
        own, out, come = held_by(u)
        for copy in rs_copies(u, t - 1):
            copy.wait_recv()
        n, at, to = 8 >> (t - 1), offset(t - 1), offset(t)
        keep = 1 if t == 2 and u < M0 else n // 2
        out[pl.ds(to, n - keep)] = (
            own[pl.ds(keep, n - keep)] + come[pl.ds(at + keep, n - keep)].astype(F32)
        ).astype(BF16)
        for copy in rs_copies(u, t):
            start(copy)
        own[pl.ds(0, keep)] = own[pl.ds(0, keep)] + come[pl.ds(at, keep)].astype(F32)

    def rs_last(u):
        own, out, come = held_by(u)
        for copy in rs_copies(u, 2 if u < M0 else 3):
            copy.wait_recv()
        value = own[0]
        for i in range(12 if u < M0 else 14, 15):
            value = value + come[i].astype(F32)
        return value

    def corrected(value, block):
        return (value + corr[block]) * jnp.concatenate([rst[block]] * 3, axis=1)

    head_gain = qkg_ref[:, half_at(0, vy)]

    def head_norm(value, which):
        parts = []
        for h in range(3):
            cut = slice(h * HD, (h + 1) * HD)
            v = value[:, cut]
            mean = jnp.mean(v, -1, keepdims=True)
            square = jnp.mean(v * v, -1, keepdims=True)
            parts.append((v - mean) * lax.rsqrt(square - mean * mean + 1e-06) * head_gain[which:which + 1, cut])
        return jnp.concatenate(parts, axis=1).astype(BF16)

    def kv_copies(c, s):
        links = KV_LINKS[c]
        if s == 0:
            parts = [(0, 1, 0, links[:1]), (0, 2, 1, links[1:2]), (0, 3, 2, links[:2])]
        else:
            parts = [(pl.ds(0, 4), pl.ds(4, 4), 3, links[2:])]
        return [
            remote(kv.at[c, at], kv.at[c, to], kv_s.at[c, i], kv_r.at[c, i], towards(*dims)) for at, to, i, dims in parts
        ]

    def ag_copies(k, i, s):
        c = i if i < 4 else A_CLASS[k]
        if i < 4:
            n = 1 << s
            parts = [(pl.ds(0, n), pl.ds(n, n), s, ((c + 3 - s) % 4,))]
        else:
            n, d, e = 1 << 2 * s, (c + 3 - 2 * s) % 4, (c + 2 - 2 * s) % 4
            parts = [
                (pl.ds(0, n), pl.ds(n * m, n), 3 * s + m - 1, dims) for m, dims in ((1, (d,)), (2, (e,)), (3, (d, e)))
            ]
        return [
            remote(agb.at[k, i, at], agb.at[k, i, to], ag_s.at[k, i, j], ag_r.at[k, i, j], towards(*dims))
            for at, to, j, dims in parts
        ]

    def ag_step(k, i, s):
        if s > 0:
            for copy in ag_copies(k, i, s - 1):
                copy.wait_recv()
        if s < (4 if i < 4 else 2):
            for copy in ag_copies(k, i, s):
                start(copy)

    def rs_end(u):
        value = rs_last(u)
        if u < Q0:
            kv[u, 0, pl.ds(0, 16)] = head_norm(corrected(value[0:16], u), 1)
            kv[u, 0, pl.ds(16, 16)] = corrected(value[16:32], 4 + u).astype(BF16)
            kv_step(u, 0)
        elif u < M0:
            qn[u - Q0] = head_norm(corrected(value, 4 + u), 0)
        else:
            k, c = (u - M0) // 4, (u - M0) % 4
            value = corrected(value, 4 + u)
            agb[k, c, 0] = (0.5 * value * (1.0 + lax.erf(value * (0.5 ** 0.5)))).astype(BF16)
            ag_step(k, c, 0)

    def kv_step(c, s):
        if s > 0:
            for copy in kv_copies(c, s - 1):
                copy.wait_recv()
        if s < 2:
            for copy in kv_copies(c, s):
                start(copy)

    def attention():
        row = lax.broadcasted_iota(jnp.int32, (48, HD), 0)
        first = (row & 15) * 24 + drow * 3 + (row >> 4) < c0
        queries = qn[...].reshape(48, 384)
        for h in range(3):
            cut = slice(h * HD, (h + 1) * HD)
            found = []
            for image in range(2):
                held = kv[pl.ds(2 * image, 2), :, :, cut]
                keys = held[:, :, 0:16].reshape(256, HD)
                values = held[:, :, 16:32].reshape(256, HD)
                scores = dot_t(queries[:, cut], keys) * HD ** (-0.5)
                expo = jnp.exp(scores - jnp.max(scores, -1, keepdims=True))
                weights = (expo / jnp.sum(expo, -1, keepdims=True)).astype(BF16)
                found.append(dot(weights, values))
            attended = jnp.where(first, found[0], found[1]).astype(BF16)
            for k in range(3):
                agb[k, 4, 0, :, cut] = attended[k * 16:(k + 1) * 16]
        for k in range(3):
            ag_step(k, 4, 0)

    begun, loaded_wd, finished = set(), set(), set()

    def branch(k, i):
        ag_step(k, i, 4 if i < 4 else 2)
        c = i if i < 4 else A_CLASS[k]
        value = None
        for h in range(2):
            left = jnp.concatenate([agb[k, i, place_of(c, b, h)] for b in range(8)], axis=0)
            if (i, h) not in loaded_wd:
                load_wd[i, h].wait()
                loaded_wd.add((i, h))
            part = dot(left, wd[i, h])
            value = part if value is None else value + part
        value = value.reshape(8, 16, 384)
        bsum[k] = bsum[k] + value if k in begun else value
        begun.add(k)

    def z_send(k):
        zs[k] = bsum[k].astype(BF16)
        for o in range(7):
            src = zs.at[k, relative(column[o])]
            start(remote(src, zr.at[k, o], z_s.at[k, o], z_r.at[k], (dp, mx, column[o])))

    def adapt(k):
        if not begun & {"a"}:
            adapter_ready()
            begun.add("a")
        remote(zr.at[k], zr.at[k], z_s.at[k, 0], z_r.at[k], (dp, mx, column[0])).wait_recv()
        value = bsum[k, relative(z)]
        for o in range(7):
            value = value + zr[k, o].astype(F32)
        updated = (xz[pl.ds(k * 16, 16)] + value).astype(BF16)
        for b in range(8):
            part = dot(updated, wa[b])
            for j in range(4):
                tr[k, pl.ds(b * 4 + j, 16, stride=32), :] = part[:, j * 128:(j + 1) * 128]
        fs[k] = tr[k].astype(BF16).reshape(16, 32, 128)
        for o in range(15):
            start(remote(fs.at[k, plane[o]], fr.at[k, o], f_s.at[k, o], f_r.at[k], (dp, plane[o], z)))

    def finish(k):
        remote(fr.at[k], fr.at[k], f_s.at[k, 0], f_r.at[k], (dp, plane[0], z)).wait_recv()
        value = tr[k, pl.ds(pl.multiple_of(mx * 32, 32), 32)]
        for o in range(15):
            value = value + fr[k, o].astype(F32)
        for b in range(32):
            res[k:k + 1, b * 128:(b + 1) * 128] = value[b:b + 1]
        finished.add(k)
        if len(finished) == 3:
            out_ref[...] = res[...].astype(BF16)

    def adapter_ready():
        for way in range(2):
            for s in range(1, 5 - way):
                across_copy(way, s).wait_recv()

    def residual():
        row = lax.broadcasted_iota(jnp.int32, (48, 128), 0)
        xz[...] = dot(pick((row & 15) * 24 + z * 3 + (row >> 4)), xb)

    def drain():
        while sent:
            sent.pop(0).wait_send()

    def greet():
        pl.semaphore_wait(barrier, len(greeted))

    events = {
        "greet": greet, "p": product, "r": rs_step, "e": rs_end, "v": kv_step, "att": attention, "g": ag_step,
        "b": branch, "z": z_send, "a": adapt, "f": finish, "w": ring_step, "s": stat_step, "c": c_step,
        "n": correct, "d": drain, "x": residual, "ch": choose,
    }
    for event in ORDER:
        events[event[0]](*event[1:])
    drain()


def per_device(patches, ln_gain, w_qkv, qk_gain, w_out, w_up, w_down, w_adapt, patch_counts):
    vmem, hbm = pl.BlockSpec(memory_space=pltpu.VMEM), pl.BlockSpec(memory_space=pl.ANY)
    dma = pltpu.SemaphoreType.DMA
    return pl.pallas_call(
        kernel,
        out_shape=jax.ShapeDtypeStruct((3, 4096), BF16),
        in_specs=[hbm, vmem, hbm, vmem, hbm, hbm, hbm, hbm, pl.BlockSpec(memory_space=pltpu.SMEM)],
        out_specs=vmem,
        scratch_shapes=[
            pltpu.VMEM((512, 384), BF16),
            pltpu.VMEM((7, 8, 16, 384), BF16),
            pltpu.VMEM((7, 2, 384, 384), BF16),
            pltpu.VMEM((5, 2, 384, 384), BF16),
            pltpu.VMEM((8, 384, 512), BF16),
            pltpu.VMEM((16, 2, 512), F32),
            pltpu.VMEM((1, 16, 384), BF16),
            pltpu.VMEM((16, 16, 384), BF16),
            pltpu.VMEM((4, 8, 16, 128), BF16),
            pltpu.VMEM((23, 16, 384), F32),
            pltpu.VMEM((23, 16, 128), F32),
            pltpu.VMEM((UNITS - Q0, 8, 16, 384), F32),
            pltpu.VMEM((UNITS - Q0, 15, 16, 384), BF16),
            pltpu.VMEM((UNITS - Q0, 15, 16, 384), BF16),
            pltpu.VMEM((Q0, 8, 32, 384), F32),
            pltpu.VMEM((Q0, 15, 32, 384), BF16),
            pltpu.VMEM((Q0, 15, 32, 384), BF16),
            pltpu.VMEM((4, 8, 32, 384), BF16),
            pltpu.VMEM((3, 16, 384), BF16),
            pltpu.VMEM((3, 5, 16, 16, 384), BF16),
            pltpu.VMEM((3, 8, 16, 384), BF16),
            pltpu.VMEM((3, 8, 16, 384), F32),
            pltpu.VMEM((3, 7, 16, 384), BF16),
            pltpu.VMEM((48, 384), F32),
            pltpu.VMEM((3, 512, 128), F32),
            pltpu.VMEM((3, 16, 32, 128), BF16),
            pltpu.VMEM((3, 15, 32, 128), BF16),
            pltpu.VMEM((3, 4096), F32),
            dma, dma((7, 2)), dma((5, 2)), dma,
            dma((6,)), dma((6,)),
            dma((6,)), dma((6,)),
            dma((UNITS, 5)), dma((UNITS, 5)),
            dma((4, 4)), dma((4, 4)),
            dma((3, 5, 6)), dma((3, 5, 6)),
            dma((3, 7)), dma((3,)),
            dma((3, 15)), dma((3,)),
            dma((7,)), dma((7,)),
            dma((7,)), dma((7,)),
        ],
        compiler_params=pltpu.CompilerParams(
            collective_id=0, has_side_effects=True, vmem_limit_bytes=60 * 2**20
        ),
    )(patches, ln_gain, w_qkv, qk_gain, w_out, w_up, w_down, w_adapt, patch_counts)


def solution(mesh):
    return jax.shard_map(
        per_device,
        mesh=mesh,
        in_specs=(
            P("dp", "mx"),
            P("mx"),
            P(None, "mx", "my"),
            P(None, "my"),
            P("my", "mx"),
            P("mx", "my"),
            P("my", "mx"),
            P("mx", "my"),
            P("dp", None),
        ),
        out_specs=P(("dp", "mx", "my"), None),
        check_vma=False,
    )
```
